512 devices in a mesh: base: 32 (over y, x), chan: 16 (over z, core).
Axes of the slice: x: 4, y: 8, z: 8, core: 2. Of those that a mesh axis runs over, the one named last changes fastest.
Arguments:
- gains: float32 [128, 8, 2048], P('base', None, 'chan'), may hold values from -6 to 6
- delays: float32 [128, 2], P('base'), may hold values from -4 to 4
- model: bfloat16 [8192, 8, 2048], P('base', None, 'chan'), may hold values from -6 to 6
- antenna1: int32 [8192], P('base'), may hold values from 0 to 126, as said below
- antenna2: int32 [8192], P('base'), may hold values from 1 to 127, as said below
- dir_band: float32 [128, 8, 2048], P('base', None, 'chan'), may hold values from -6 to 6
- dir_delay: float32 [128, 2], P('base'), may hold values from -6 to 6
- res_band: float32 [128, 8, 2048], P('base', None, 'chan'), may hold values from -6 to 6
- res_delay: float32 [128, 2], P('base'), may hold values from -6 to 6
- iter_band: float32 [128, 8, 2048], P('base', None, 'chan'), may hold values from -6 to 6
- iter_delay: float32 [128, 2], P('base'), may hold values from -6 to 6
Outputs:
- new_iter_band: float32 [128, 8, 2048], P('base', None, 'chan')
- new_iter_delay: float32 [128, 2], P('base')
- new_res_band: float32 [128, 8, 2048], P('base', None, 'chan')
- new_res_delay: float32 [128, 2], P('base')
- new_dir_band: float32 [128, 8, 2048], P('base', None, 'chan')
- new_dir_delay: float32 [128, 2], P('base')
The draws below stay inside these ranges and needn't reach their ends.
Inputs may be any that keep to these rules, and one draw needn't show every extreme that they name: antenna1[b] < antenna2[b]. Stations are in blocks of 4 consecutive numbers; the baselines in rows d * 256 to (d + 1) * 256 - 1 have one station in block d and the other in block d, d + 1, d - 1 or d plus half the number of blocks (modulo the number of blocks). `antenna2`: as for antenna1.
All inputs are finite; a program needn't handle non-finite values.
Results may differ from the reference program's by a relative error of at most 0.0003.
Values sent between devices are 32-bit elements; how exact they have to be, the bound alone decides.
No kernel may reach another device: no remote copies, remote signals or barrier semaphores. Data moves between devices by JAX's collectives and lax.ppermute only.
A program may use at most 64 MiB of HBM per device.

```python
import math
import jax
import jax.numpy as jnp
from jax import lax

ANTENNAS_SHARE = 4
PAIRS_PER_SHARE = 256
C_DEV = 128
STATIONS = 128
PAIRS_OVERALL = 8192
CHANNEL_TOTAL = 2048
N_CHAN = 16


def station_pairs(key):
    segment_sequence = PAIRS_OVERALL // PAIRS_PER_SHARE
    entry_tally = jnp.arange(PAIRS_OVERALL, dtype=jnp.int32)
    holder_segment = entry_tally // PAIRS_PER_SHARE
    within_share_entry = entry_tally % PAIRS_PER_SHARE
    row_kind = within_share_entry % 4
    leading_key, offset_key, cross_key = jax.random.split(key, 3)
    leading_selector = jax.random.randint(leading_key, (PAIRS_OVERALL,), 0, ANTENNAS_SHARE, dtype=jnp.int32)
    offset_selector = jax.random.randint(offset_key, (PAIRS_OVERALL,), 1, ANTENNAS_SHARE, dtype=jnp.int32)
    cross_selector = jax.random.randint(cross_key, (PAIRS_OVERALL,), 0, ANTENNAS_SHARE, dtype=jnp.int32)
    own_second = (leading_selector + offset_selector) % ANTENNAS_SHARE
    block_offset = jnp.where(row_kind == 1, 1, jnp.where(row_kind == 2, segment_sequence // 2, segment_sequence - 1))
    other_block = (holder_segment + block_offset) % segment_sequence
    station_one = holder_segment * ANTENNAS_SHARE + leading_selector
    station_two = jnp.where(row_kind == 0, holder_segment * ANTENNAS_SHARE + own_second, other_block * ANTENNAS_SHARE + cross_selector)
    forced_high = within_share_entry == 0
    forced_low = within_share_entry == 4
    station_one = jnp.where(forced_high, holder_segment * ANTENNAS_SHARE + ANTENNAS_SHARE - 2, jnp.where(forced_low, holder_segment * ANTENNAS_SHARE, station_one))
    station_two = jnp.where(forced_high, holder_segment * ANTENNAS_SHARE + ANTENNAS_SHARE - 1, jnp.where(forced_low, holder_segment * ANTENNAS_SHARE + 1, station_two))
    lower = jnp.minimum(station_one, station_two).astype(jnp.int32)
    upper = jnp.maximum(station_one, station_two).astype(jnp.int32)
    return (lower, upper)


def draw_antenna1(key, part):
    return station_pairs(key)[0]


def draw_antenna2(key, part):
    return station_pairs(key)[1]


def levels(key, extent, cuts, low, high):
    def one(dim, shards_of):
        draws = jax.random.uniform(jax.random.fold_in(jax.random.fold_in(key, 6), dim), (shards_of,), jnp.float32, low / len(cuts), high / len(cuts))
        return jnp.repeat(jnp.exp(draws), extent[dim] // shards_of).reshape((-1,) + (1,) * (len(extent) - dim - 1))

    factor_of = one(*cuts[0])
    for cut in cuts[1:]:
        factor_of = factor_of * one(*cut)
    return factor_of


def bell_draw(rng, shape, deviation, limit, shards=(), held_as=jnp.bfloat16):
    result = jax.random.normal(rng, shape, jnp.float32) * deviation
    if len(shards) > 0:
        result = levels(rng, shape, shards, -0.22, 0.18) * result
    return jnp.clip(result, min=-limit, max=limit).astype(held_as)


def setup_inputs(seed: int = 0) -> dict:
    key_of = jax.random.split(jax.random.key(seed), 12)
    return {
        "gains": bell_draw(key_of[0], (STATIONS, 8, CHANNEL_TOTAL), 1.0, 6.0, ((0, 32), (2, 16)), jnp.float32),
        "delays": jnp.clip(jax.random.uniform(key_of[1], (STATIONS, 2), jnp.float32, -4.0, 4.0) * levels(key_of[1], (STATIONS, 2), ((0, 32),), -0.4, 0.0), -4.0, 4.0),
        "model": bell_draw(key_of[2], (PAIRS_OVERALL, 8, CHANNEL_TOTAL), 1.0, 6.0, ((0, 32), (2, 16))),
        "antenna1": draw_antenna1(jax.random.fold_in(key_of[11], 71), 0),
        "antenna2": draw_antenna2(jax.random.fold_in(key_of[11], 71), 0),
        "dir_band": bell_draw(key_of[5], (STATIONS, 8, CHANNEL_TOTAL), 1.0, 6.0, ((0, 32), (2, 16)), jnp.float32),
        "dir_delay": bell_draw(key_of[6], (STATIONS, 2), 1.0, 6.0, ((0, 32),), jnp.float32),
        "res_band": bell_draw(key_of[7], (STATIONS, 8, CHANNEL_TOTAL), 1.0, 6.0, ((0, 32), (2, 16)), jnp.float32),
        "res_delay": bell_draw(key_of[8], (STATIONS, 2), 1.0, 6.0, ((0, 32),), jnp.float32),
        "iter_band": bell_draw(key_of[9], (STATIONS, 8, CHANNEL_TOTAL), 1.0, 6.0, ((0, 32), (2, 16)), jnp.float32),
        "iter_delay": bell_draw(key_of[10], (STATIONS, 2), 1.0, 6.0, ((0, 32),), jnp.float32),
    }


full_turn = 2.0 * math.pi
damping_weight = 0.5

def split_parts(packed):
    count = packed.shape[0]
    width = packed.shape[-1]
    return (packed[:, :4].reshape(count, 2, 2, width), packed[:, 4:].reshape(count, 2, 2, width))

def join_parts(real, imag):
    count = real.shape[0]
    width = real.shape[-1]
    return jnp.concatenate([real.reshape(count, 4, width), imag.reshape(count, 4, width)], axis=1)

def matrix_product(left, right):
    return left[:, :, 0:1, :] * right[:, None, 0, :, :] + left[:, :, 1:2, :] * right[:, None, 1, :, :]

def complex_product(left, right):
    real = matrix_product(left[0], right[0]) - matrix_product(left[1], right[1])
    imag = matrix_product(left[0], right[1]) + matrix_product(left[1], right[0])
    return (real, imag)

def adjoint(pair):
    return (jnp.swapaxes(pair[0], 1, 2), -jnp.swapaxes(pair[1], 1, 2))

def station_terms(gains, delays, dir_band, dir_delay, freq, delay_scale):
    phase = full_turn * delays[:, :, None] * freq[None, None, :]
    cosine = jnp.cos(phase)[:, None, :, :]
    sine = jnp.sin(phase)[:, None, :, :]
    gain_re, gain_im = split_parts(gains)
    jones_re = cosine * gain_re - sine * gain_im
    jones_im = cosine * gain_im + sine * gain_re
    move_re, move_im = split_parts(dir_band)
    turned_re = cosine * move_re - sine * move_im
    turned_im = cosine * move_im + sine * move_re
    rate = full_turn * delay_scale * dir_delay[:, :, None] * freq[None, None, :]
    rate = rate[:, None, :, :]
    tangent_re = turned_re - rate * jones_im
    tangent_im = turned_im + rate * jones_re
    return (join_parts(jones_re, jones_im), join_parts(tangent_re, tangent_im), cosine, sine)

def baseline_change(jones_p, tangent_p, jones_q, tangent_q, model, multiplier_factor):
    model_pair = split_parts(model)
    right_q = complex_product(model_pair, adjoint(split_parts(jones_q)))
    left_p = complex_product(split_parts(jones_p), model_pair)
    first = complex_product(split_parts(tangent_p), right_q)
    second = complex_product(left_p, adjoint(split_parts(tangent_q)))
    change = join_parts(multiplier_factor * (first[0] + second[0]), multiplier_factor * (first[1] + second[1]))
    return (change, right_q, left_p)

def reference(gains, delays, model, antenna1, antenna2, dir_band, dir_delay, res_band, res_delay, iter_band, iter_delay):
    channels = C_DEV * N_CHAN
    stations = gains.shape[0]
    multiplier_factor = (ANTENNAS_SHARE / (2.0 * PAIRS_PER_SHARE)) ** 0.5
    delay_scale = channels ** (-0.5)

    def block(carry, index):
        start = index * C_DEV
        freq = ((start + jnp.arange(C_DEV, dtype=jnp.int32)).astype(jnp.float32) + 0.5) / channels - 0.5
        gain_block = lax.dynamic_slice_in_dim(gains, start, C_DEV, 2)
        model_block = lax.dynamic_slice_in_dim(model, start, C_DEV, 2).astype(jnp.float32)
        band_block = lax.dynamic_slice_in_dim(dir_band, start, C_DEV, 2)

        def change_of(band, delay):
            jones, tangent, cosine, sine = station_terms(gain_block, delays, band, delay, freq, delay_scale)
            return baseline_change(jones[antenna1], tangent[antenna1], jones[antenna2], tangent[antenna2], model_block, multiplier_factor)[0]
        change, pullback = jax.vjp(change_of, band_block, dir_delay)
        grad_band, grad_delay = pullback(change)
        return (carry + grad_delay, grad_band)
    grad_delay, bands = lax.scan(block, jnp.zeros((stations, 2), jnp.float32), jnp.arange(N_CHAN, dtype=jnp.int32))
    grad_band = jnp.transpose(bands, (1, 2, 0, 3)).reshape(stations, 8, channels)
    curv_band = grad_band + damping_weight * dir_band
    curv_delay = grad_delay + damping_weight * dir_delay
    squares = jnp.sum(res_band * res_band) + jnp.sum(res_delay * res_delay)
    curvature = jnp.sum(dir_band * curv_band) + jnp.sum(dir_delay * curv_delay)
    alpha = squares / curvature
    new_iter_band = iter_band + alpha * dir_band
    new_iter_delay = iter_delay + alpha * dir_delay
    new_res_band = res_band - alpha * curv_band
    new_res_delay = res_delay - alpha * curv_delay
    fresh = jnp.sum(new_res_band * new_res_band) + jnp.sum(new_res_delay * new_res_delay)
    ratio = fresh / squares
    new_dir_band = new_res_band + ratio * dir_band
    new_dir_delay = new_res_delay + ratio * dir_delay
    return (new_iter_band, new_iter_delay, new_res_band, new_res_delay, new_dir_band, new_dir_delay)
```

```python
import math

import jax
import jax.numpy as jnp
from jax import lax
from jax.experimental import pallas as pl
from jax.experimental.pallas import tpu as pltpu
from jax.sharding import Mesh
from jax.sharding import PartitionSpec as P

full_turn = 2.0 * math.pi
damping_weight = 0.5

f32 = jnp.float32
bf16 = jnp.bfloat16


def vmem():
    return pl.BlockSpec(memory_space=pltpu.VMEM)


def smem():
    return pl.BlockSpec(memory_space=pltpu.SMEM)


def params(mib):
    return pltpu.CompilerParams(vmem_limit_bytes=mib * 1024 * 1024)


def shape(*dims, dtype=f32):
    return jax.ShapeDtypeStruct(dims, dtype)


def frequencies(chan, width, channels):
    index = lax.broadcasted_iota(jnp.int32, (1, width), 1) + chan * width
    return (index.astype(f32) + 0.5) / channels - 0.5


def column(row_ref):
    count = row_ref.shape[1]
    eye = lax.broadcasted_iota(jnp.int32, (count, count), 0) == lax.broadcasted_iota(
        jnp.int32, (count, count), 1
    )
    parts = [
        jnp.sum(
            jnp.where(eye, jnp.broadcast_to(row_ref[a : a + 1, :], (count, count)), 0.0),
            axis=1,
            keepdims=True,
        )
        for a in range(2)
    ]
    return jnp.concatenate(parts, axis=0)


def station_kernel(
    chan_ref, gains_ref, band_ref, delays_ref, move_ref, terms_ref, turn_ref, packed, *, channels
):
    owned, _, width = gains_ref.shape
    half = 2 * owned
    delay_scale = channels ** (-0.5)
    freq = frequencies(chan_ref[0], width, channels)
    phase = full_turn * column(delays_ref) * freq
    rate = full_turn * delay_scale * column(move_ref) * freq
    cosine = jnp.cos(phase)
    sine = jnp.sin(phase)
    turn_ref[0:half, :] = cosine
    turn_ref[half : 2 * half, :] = sine
    for j in range(8):
        packed[j * owned : (j + 1) * owned, :] = gains_ref[:, j, :]
        packed[(8 + j) * owned : (9 + j) * owned, :] = band_ref[:, j, :]
    for r in range(2):
        re = slice(r * half, (r + 1) * half)
        im = slice((2 + r) * half, (3 + r) * half)
        move_re = slice((4 + r) * half, (5 + r) * half)
        move_im = slice((6 + r) * half, (7 + r) * half)
        jones_re = cosine * packed[re, :] - sine * packed[im, :]
        jones_im = cosine * packed[im, :] + sine * packed[re, :]
        terms_ref[re, :] = jones_re
        terms_ref[im, :] = jones_im
        terms_ref[move_re, :] = (
            cosine * packed[move_re, :] - sine * packed[move_im, :] - rate * jones_im
        )
        terms_ref[move_im, :] = (
            cosine * packed[move_im, :] + sine * packed[move_re, :] + rate * jones_re
        )


def prepare_kernel(block_ref, model_ref, first_ref, second_ref, model_out, gather_out, scatter_out, *, owned, blocks):
    rows = first_ref.shape[1]
    width = model_ref.shape[1]
    group = 32
    block = block_ref[0]
    size = 8 * group
    out_row = lax.broadcasted_iota(jnp.int32, (size, size), 0)
    in_row = lax.broadcasted_iota(jnp.int32, (size, size), 1)
    wanted = (out_row % group) * 8 + out_row // group
    shuffle = jnp.where(in_row == wanted, 1.0, 0.0).astype(bf16)
    for g in range(rows // group):
        part = jnp.dot(
            shuffle, model_ref[g * size : (g + 1) * size, :], preferred_element_type=f32
        )
        for j in range(8):
            model_out[j, g * group : (g + 1) * group, :] = part[j * group : (j + 1) * group, :]
    slots = 4 * owned
    slot = lax.broadcasted_iota(jnp.int32, (slots, 2 * rows), 0)
    kind = slot // owned
    offset = jnp.where(kind == 0, 0, jnp.where(kind == 1, 1, jnp.where(kind == 2, blocks - 1, blocks // 2)))
    station = ((block + offset) % blocks) * owned + slot % owned
    both = jnp.concatenate([first_ref[...], second_ref[...]], axis=1)
    pick = jnp.where(station == both, 1.0, 0.0)
    scatter_out[...] = pick.astype(bf16)
    filled = jnp.concatenate([pick] * 3 + [jnp.zeros((128 - 3 * slots, 2 * rows), f32)], axis=0)
    gather_out[...] = jnp.transpose(filled).astype(bf16)


def times(a, b):
    out = []
    for r in range(2):
        for c in range(2):
            out.append(
                a[r * 2] * b[c] - a[4 + r * 2] * b[4 + c] + a[r * 2 + 1] * b[2 + c] - a[5 + r * 2] * b[6 + c]
            )
    for r in range(2):
        for c in range(2):
            out.append(
                a[r * 2] * b[4 + c] + a[4 + r * 2] * b[c] + a[r * 2 + 1] * b[6 + c] + a[5 + r * 2] * b[2 + c]
            )
    return out


def times_adjoint(a, b):
    out = []
    for r in range(2):
        for c in range(2):
            out.append(
                a[r * 2] * b[c * 2]
                + a[4 + r * 2] * b[4 + c * 2]
                + a[r * 2 + 1] * b[c * 2 + 1]
                + a[5 + r * 2] * b[5 + c * 2]
            )
    for r in range(2):
        for c in range(2):
            out.append(
                a[4 + r * 2] * b[c * 2]
                - a[r * 2] * b[4 + c * 2]
                + a[5 + r * 2] * b[c * 2 + 1]
                - a[r * 2 + 1] * b[5 + c * 2]
            )
    return out


def adjoint_times(a, b):
    out = []
    for r in range(2):
        for c in range(2):
            out.append(
                a[r] * b[c] + a[4 + r] * b[4 + c] + a[2 + r] * b[2 + c] + a[6 + r] * b[6 + c]
            )
    for r in range(2):
        for c in range(2):
            out.append(
                a[r] * b[4 + c] - a[4 + r] * b[c] + a[2 + r] * b[6 + c] - a[6 + r] * b[2 + c]
            )
    return out


def baseline_kernel(
    own_ref, next_ref, last_ref, far_ref, model_ref, gather_ref, scatter_ref,
    own_out, next_out, last_out, far_out, table, picked, grads, *, factor
):
    _, rows, width = model_ref.shape
    slots = table.shape[0]
    owned = slots // 4
    for k, ref in enumerate((own_ref, next_ref, last_ref, far_ref)):
        for j in range(16):
            table[k * owned : (k + 1) * owned, j * width : (j + 1) * width] = ref[
                j * owned : (j + 1) * owned, :
            ]
    exact = table[...]
    high = exact.astype(bf16)
    rest = exact - high.astype(f32)
    middle = rest.astype(bf16)
    low = (rest - middle.astype(f32)).astype(bf16)
    split = jnp.concatenate(
        [high, middle, low, jnp.zeros((128 - 3 * slots, exact.shape[1]), bf16)], axis=0
    )
    pick = gather_ref[...]
    step = 2 * width
    for n in range(0, 16 * width, step):
        picked[:, n : n + step] = jnp.dot(pick, split[:, n : n + step], preferred_element_type=f32)

    def chunk(i, carry):
        at = pl.ds(pl.multiple_of(i * 8, 8), 8)
        at_q = pl.ds(pl.multiple_of(rows + i * 8, 8), 8)
        cols = [slice(j * width, (j + 1) * width) for j in range(16)]
        model = [model_ref[j, at, :] for j in range(8)]
        right = times_adjoint(model, [picked[at_q, c] for c in cols[:8]])
        left = times([picked[at, c] for c in cols[:8]], model)
        one = times([picked[at, c] for c in cols[8:]], right)
        two = times_adjoint(left, [picked[at_q, c] for c in cols[8:]])
        change = [a + b for a, b in zip(one, two)]
        for c, value in zip(cols, times_adjoint(change, right)):
            grads[at, c] = value
        for c, value in zip(cols, adjoint_times(change, left)):
            grads[at_q, c] = value
        return carry

    lax.fori_loop(0, rows // 8, chunk, 0, unroll=2)
    sums = []
    for n in range(0, 8 * width, step):
        value = grads[:, n : n + step]
        high = value.astype(bf16)
        low = (value - high.astype(f32)).astype(bf16)
        total = jnp.dot(scatter_ref[...], high, preferred_element_type=f32) + jnp.dot(
            scatter_ref[...], low, preferred_element_type=f32
        )
        table[:, n : n + step] = factor * total
    for k, ref in enumerate((own_out, next_out, last_out, far_out)):
        for j in range(8):
            ref[j * owned : (j + 1) * owned, :] = table[
                k * owned : (k + 1) * owned, j * width : (j + 1) * width
            ]


def curvature_kernel(
    place_ref, own_ref, a_ref, b_ref, c_ref, terms_ref, turn_ref, band_ref, res_ref, delay_ref, res_delay_ref,
    curv_ref, row_ref, *, channels
):
    owned, _, width = band_ref.shape
    half = 2 * owned
    delay_scale = channels ** (-0.5)
    freq = frequencies(place_ref[0], width, channels)
    cosine = turn_ref[0:half, :]
    sine = turn_ref[half : 2 * half, :]
    total = own_ref[...] + a_ref[...] + b_ref[...] + c_ref[...]
    moved = jnp.zeros((half, width), f32)
    for r in range(2):
        re = slice(r * half, (r + 1) * half)
        im = slice((2 + r) * half, (3 + r) * half)
        grad_re, grad_im = total[re, :], total[im, :]
        moved = moved + (terms_ref[re, :] * grad_im - terms_ref[im, :] * grad_re)
        band_re = cosine * grad_re + sine * grad_im
        band_im = cosine * grad_im - sine * grad_re
        for a in range(2):
            rows = slice(a * owned, (a + 1) * owned)
            j = 2 * r + a
            curv_ref[:, j, :] = band_re[rows, :] + damping_weight * band_ref[:, j, :]
            curv_ref[:, 4 + j, :] = band_im[rows, :] + damping_weight * band_ref[:, 4 + j, :]
    moved = jnp.sum(moved * (full_turn * delay_scale * freq), axis=1, keepdims=True)
    curv, band, res = curv_ref[...], band_ref[...], res_ref[...]
    scalars = [
        jnp.sum(jnp.sum(jnp.sum(x, axis=0), axis=0, keepdims=True), axis=1, keepdims=True)
        for x in (res * res, res * curv, curv * curv, band * curv)
    ]
    here = jnp.where(place_ref[1] == 0, 1.0, 0.0)
    values = jnp.concatenate(
        [moved] + scalars + [jnp.zeros((4, 1), f32)]
        + [here * column(delay_ref), here * column(res_delay_ref)],
        axis=0,
    )
    count = values.shape[0]
    diagonal = lax.broadcasted_iota(jnp.int32, (count, width), 0) == lax.broadcasted_iota(
        jnp.int32, (count, width), 1
    )
    row = jnp.sum(
        jnp.where(diagonal, jnp.broadcast_to(values, (count, width)), 0.0), axis=0, keepdims=True
    )
    row_ref[...] = jnp.broadcast_to(row, row_ref.shape)


def update_kernel(
    block_ref, rows_ref, curv_ref, band_ref, res_ref, iter_ref, delay_ref, res_delay_ref, iter_delay_ref,
    iter_out, iter_delay_out, res_out, res_delay_out, dir_out, dir_delay_out
):
    rows = rows_ref[...]
    count, width = rows.shape
    owned = band_ref.shape[0]
    half = 2 * owned
    sums = jnp.sum(rows, axis=0, keepdims=True)
    lane = lax.broadcasted_iota(jnp.int32, (1, width), 1)

    def scalar(x):
        return jnp.sum(x, axis=1, keepdims=True)

    pair = rows + pltpu.roll(rows, count - 1, 0)
    moves = pltpu.roll(rows, width - 16, 1)
    lefts = pltpu.roll(rows, width - 24, 1)
    curves = pair + damping_weight * moves
    valid = (lax.broadcasted_iota(jnp.int32, (count, width), 0) % 2 == 0) & (
        lax.broadcasted_iota(jnp.int32, (count, width), 1) < half
    )

    def delays(x):
        return scalar(jnp.sum(jnp.where(valid, x, 0.0), axis=0, keepdims=True))

    squares = scalar(jnp.where(lane == half, sums, 0.0)) + delays(lefts * lefts)
    cross = scalar(jnp.where(lane == half + 1, sums, 0.0)) + delays(lefts * curves)
    norm = scalar(jnp.where(lane == half + 2, sums, 0.0)) + delays(curves * curves)
    curvature = scalar(jnp.where(lane == half + 3, sums, 0.0)) + delays(moves * curves)
    alpha = squares / curvature
    fresh = squares + alpha * (alpha * norm - 2.0 * cross)
    ratio = fresh / squares

    band, curv = band_ref[...], curv_ref[...]
    alpha3 = alpha.reshape(1, 1, 1)
    ratio3 = ratio.reshape(1, 1, 1)
    iter_out[...] = iter_ref[...] + alpha3 * band
    new_res = res_ref[...] - alpha3 * curv
    res_out[...] = new_res
    dir_out[...] = new_res + ratio3 * band

    mine = lax.broadcasted_iota(jnp.int32, (count, width), 0) == 2 * block_ref[0]
    own = jnp.sum(jnp.where(mine, pair, 0.0), axis=0, keepdims=True)
    own = jnp.concatenate([own[:, 0:owned], own[:, owned:half]], axis=0)
    move = delay_ref[...]
    iter_delay_out[...] = iter_delay_ref[...] + alpha * move
    new_left = res_delay_ref[...] - alpha * (own + damping_weight * move)
    res_delay_out[...] = new_left
    dir_delay_out[...] = new_left + ratio * move


def body(
    gains,
    delays,
    model,
    antenna1,
    antenna2,
    dir_band,
    dir_delay,
    res_band,
    res_delay,
    iter_band,
    iter_delay,
):
    owned, _, width = gains.shape
    rows = model.shape[0]
    blocks = lax.axis_size("base")
    lines = lax.axis_size("z")
    cores = lax.axis_size("core")
    channels = width * lines * cores
    slots = 4 * owned
    factor = owned / (2.0 * rows)
    block = lax.axis_index("base").astype(jnp.int32)
    chan = (lax.axis_index("z") * cores + lax.axis_index("core")).astype(jnp.int32)
    block_one = block.reshape(1)
    place = jnp.stack([chan, lax.axis_index("z").astype(jnp.int32)])

    delays_t, dir_delay_t, res_delay_t, iter_delay_t = (
        jnp.transpose(x) for x in (delays, dir_delay, res_delay, iter_delay)
    )

    terms, turn = pl.pallas_call(
        lambda *refs: station_kernel(*refs, channels=channels),
        out_shape=(shape(16 * owned, width), shape(4 * owned, width)),
        in_specs=[smem()] + [vmem()] * 4,
        out_specs=(vmem(), vmem()),
        scratch_shapes=[pltpu.VMEM((16 * owned, width), f32)],
        compiler_params=params(4),
        name="station_terms",
    )(place, gains, dir_band, delays_t, dir_delay_t)

    def step(value, by):
        return lax.ppermute(value, "base", [(i, (i + by) % blocks) for i in range(blocks)])

    near_next, near_last, far = step(terms, -1), step(terms, 1), step(terms, blocks // 2)

    model_parts, gather, scatter = pl.pallas_call(
        lambda *refs: prepare_kernel(*refs, owned=owned, blocks=blocks),
        out_shape=(
            shape(8, rows, width),
            shape(2 * rows, 128, dtype=bf16),
            shape(slots, 2 * rows, dtype=bf16),
        ),
        in_specs=[smem()] + [vmem()] * 3,
        out_specs=(vmem(),) * 3,
        compiler_params=params(8),
        cost_estimate=pl.CostEstimate(flops=300000000, bytes_accessed=2000000, transcendentals=0),
        name="prepare",
    )(block_one, model.reshape(rows * 8, width), antenna1.reshape(1, rows), antenna2.reshape(1, rows))

    own, to_next, to_last, to_far = pl.pallas_call(
        lambda *refs: baseline_kernel(*refs, factor=factor),
        out_shape=(shape(8 * owned, width),) * 4,
        in_specs=[vmem()] * 7,
        out_specs=(vmem(),) * 4,
        scratch_shapes=[
            pltpu.VMEM((slots, 16 * width), f32),
            pltpu.VMEM((2 * rows, 16 * width), f32),
            pltpu.VMEM((2 * rows, 8 * width), f32),
        ],
        compiler_params=params(24),
        name="baselines",
    )(terms, near_next, near_last, far, model_parts, gather, scatter)

    from_last, from_next, from_far = step(to_next, 1), step(to_last, -1), step(to_far, blocks // 2)

    curv, row = pl.pallas_call(
        lambda *refs: curvature_kernel(*refs, channels=channels),
        out_shape=(shape(owned, 8, width), shape(lines, width)),
        in_specs=[smem()] + [vmem()] * 10,
        out_specs=(vmem(), vmem()),
        compiler_params=params(4),
        name="curvature",
    )(place, own, from_last, from_next, from_far, terms, turn, dir_band, res_band, dir_delay_t, res_delay_t)

    line = lax.all_to_all(row, "z", 0, 0, tiled=True)
    peers = blocks * cores
    line = jnp.broadcast_to(jnp.sum(line, axis=0, keepdims=True), (peers, width))
    everyone = lax.all_to_all(line, ("base", "core"), 0, 0, tiled=True)

    outs = pl.pallas_call(
        update_kernel,
        out_shape=(
            shape(owned, 8, width),
            shape(2, owned),
            shape(owned, 8, width),
            shape(2, owned),
            shape(owned, 8, width),
            shape(2, owned),
        ),
        in_specs=[smem()] + [vmem()] * 8,
        out_specs=(vmem(),) * 6,
        compiler_params=params(4),
        name="update",
    )(block_one, everyone, curv, dir_band, res_band, iter_band, dir_delay_t, res_delay_t, iter_delay_t)
    return (
        outs[0],
        jnp.transpose(outs[1]),
        outs[2],
        jnp.transpose(outs[3]),
        outs[4],
        jnp.transpose(outs[5]),
    )


def solution(mesh):
    cores = 2
    blocks, chans = mesh.shape["base"], mesh.shape["chan"]
    split = Mesh(mesh.devices.reshape(blocks, chans // cores, cores), ("base", "z", "core"))
    band = P("base", None, ("z", "core"))
    delay = P("base", None)
    one = P("base")
    return jax.shard_map(
        body,
        mesh=split,
        in_specs=(band, delay, band, one, one, band, delay, band, delay, band, delay),
        out_specs=(band, delay) * 3,
        check_vma=False,
    )
```

```python
import math

import jax
import jax.numpy as jnp
from jax import lax
from jax.experimental import pallas as pl
from jax.experimental.pallas import tpu as pltpu
from jax.sharding import Mesh
from jax.sharding import PartitionSpec as P

full_turn = 2.0 * math.pi
damping_weight = 0.5

f32 = jnp.float32
bf16 = jnp.bfloat16


def vmem():
    return pl.BlockSpec(memory_space=pltpu.VMEM)


def hbm():
    return pl.BlockSpec(memory_space=pltpu.HBM)


def params(mib):
    return pltpu.CompilerParams(vmem_limit_bytes=int(mib * 1024 * 1024))


def shape(*dims, dtype=f32):
    return jax.ShapeDtypeStruct(dims, dtype)


def chan_index():
    return lax.axis_index("z") * lax.axis_size("core") + lax.axis_index("core")


def frequencies(chan, width, channels):
    index = lax.broadcasted_iota(jnp.int32, (1, width), 1) + chan * width
    return (index.astype(f32) + 0.5) / channels - 0.5


def column(row_ref):
    count = row_ref.shape[1]
    eye = lax.broadcasted_iota(jnp.int32, (count, count), 0) == lax.broadcasted_iota(
        jnp.int32, (count, count), 1
    )
    parts = [
        jnp.sum(
            jnp.where(eye, jnp.broadcast_to(row_ref[a : a + 1, :], (count, count)), 0.0),
            axis=1,
            keepdims=True,
        )
        for a in range(2)
    ]
    return jnp.concatenate(parts, axis=0)


def pick_stations(ids, gather_ref, scatter_ref, *, owned, blocks):
    rows = ids.shape[1]
    slots = 4 * owned
    slot = lax.broadcasted_iota(jnp.int32, (slots, 2 * rows), 0)
    kind = slot // owned
    block = lax.axis_index("base")
    turn_up = 1 - 2 * (block % 2)
    offset = jnp.where(kind == 0, 0, jnp.where(kind == 1, turn_up, jnp.where(kind == 2, -turn_up, blocks // 2)))
    station = ((block + offset + blocks) % blocks) * owned + slot % owned
    both = jnp.concatenate([ids[0:1, :], ids[1:2, :]], axis=1)
    pick = jnp.where(station == both, 1.0, 0.0)
    filled = jnp.concatenate([pick] * 3 + [jnp.zeros((128 - 3 * slots, 2 * rows), f32)], axis=0)
    scatter_ref[...] = pick.astype(bf16)
    gather_ref[...] = jnp.transpose(filled).astype(bf16)


def station_kernel(
    gains_hbm, band_hbm, delays_hbm, move_hbm, left_hbm, iter_hbm, first_hbm, second_hbm, model_hbm,
    terms_ref, turn_ref, small_ref, gather_ref, scatter_ref, model_ref,
    gains_ref, band_ref, delays_ref, ids, packed, sems, *, channels, blocks
):
    owned, _, width = gains_ref.shape
    half = 2 * owned
    pairs = [
        (first_hbm, ids.at[0:1]),
        (second_hbm, ids.at[1:2]),
        (delays_hbm, delays_ref),
        (move_hbm, small_ref.at[0]),
        (gains_hbm, gains_ref),
        (band_hbm, band_ref),
        (model_hbm, model_ref),
        (left_hbm, small_ref.at[1]),
        (iter_hbm, small_ref.at[2]),
    ]
    copies = [pltpu.make_async_copy(a, b, sems.at[k]) for k, (a, b) in enumerate(pairs)]
    for copy in copies:
        copy.start()
    copies[0].wait()
    copies[1].wait()
    pick_stations(ids, gather_ref, scatter_ref, owned=owned, blocks=blocks)
    copies[2].wait()
    copies[3].wait()
    delay_scale = channels ** (-0.5)
    freq = frequencies(chan_index(), width, channels)
    phase = full_turn * column(delays_ref) * freq
    rate = full_turn * delay_scale * column(small_ref.at[0]) * freq
    cosine = jnp.cos(phase)
    sine = jnp.sin(phase)
    turn_ref[0:half, :] = cosine
    turn_ref[half : 2 * half, :] = sine
    copies[4].wait()
    copies[5].wait()
    for j in range(8):
        packed[j * owned : (j + 1) * owned, :] = gains_ref[:, j, :]
        packed[(8 + j) * owned : (9 + j) * owned, :] = band_ref[:, j, :]
    for r in range(2):
        re = slice(r * half, (r + 1) * half)
        im = slice((2 + r) * half, (3 + r) * half)
        move_re = slice((4 + r) * half, (5 + r) * half)
        move_im = slice((6 + r) * half, (7 + r) * half)
        jones_re = cosine * packed[re, :] - sine * packed[im, :]
        jones_im = cosine * packed[im, :] + sine * packed[re, :]
        terms_ref[re, :] = jones_re
        terms_ref[im, :] = jones_im
        terms_ref[move_re, :] = (
            cosine * packed[move_re, :] - sine * packed[move_im, :] - rate * jones_im
        )
        terms_ref[move_im, :] = (
            cosine * packed[move_im, :] + sine * packed[move_re, :] + rate * jones_re
        )
    for copy in copies[6:]:
        copy.wait()


def times(a, b):
    out = []
    for r in range(2):
        for c in range(2):
            out.append(
                a[r * 2] * b[c] - a[4 + r * 2] * b[4 + c] + a[r * 2 + 1] * b[2 + c] - a[5 + r * 2] * b[6 + c]
            )
    for r in range(2):
        for c in range(2):
            out.append(
                a[r * 2] * b[4 + c] + a[4 + r * 2] * b[c] + a[r * 2 + 1] * b[6 + c] + a[5 + r * 2] * b[2 + c]
            )
    return out


def times_adjoint(a, b):
    out = []
    for r in range(2):
        for c in range(2):
            out.append(
                a[r * 2] * b[c * 2]
                + a[4 + r * 2] * b[4 + c * 2]
                + a[r * 2 + 1] * b[c * 2 + 1]
                + a[5 + r * 2] * b[5 + c * 2]
            )
    for r in range(2):
        for c in range(2):
            out.append(
                a[4 + r * 2] * b[c * 2]
                - a[r * 2] * b[4 + c * 2]
                + a[5 + r * 2] * b[c * 2 + 1]
                - a[r * 2 + 1] * b[5 + c * 2]
            )
    return out


def adjoint_times(a, b):
    out = []
    for r in range(2):
        for c in range(2):
            out.append(
                a[r] * b[c] + a[4 + r] * b[4 + c] + a[2 + r] * b[2 + c] + a[6 + r] * b[6 + c]
            )
    for r in range(2):
        for c in range(2):
            out.append(
                a[r] * b[4 + c] - a[4 + r] * b[c] + a[2 + r] * b[6 + c] - a[6 + r] * b[2 + c]
            )
    return out


def baseline_kernel(
    own_ref, even_ref, odd_ref, far_ref, model_ref, gather_ref, scatter_ref,
    own_out, even_out, odd_out, far_out, table, picked, grads, model_parts, *, factor
):
    _, rows, width = model_parts.shape
    slots = table.shape[0]
    owned = slots // 4
    group = 32
    size = 8 * group
    pick, scatter = gather_ref[...], scatter_ref[...]
    partner = odd_ref.at[lax.axis_index("base") % 2]
    for k, ref in enumerate((own_ref, even_ref, partner, far_ref)):
        for j in range(16):
            table[k * owned : (k + 1) * owned, j * width : (j + 1) * width] = ref[
                j * owned : (j + 1) * owned, :
            ]
    exact = table[...]
    high = exact.astype(bf16)
    rest = exact - high.astype(f32)
    middle = rest.astype(bf16)
    low = (rest - middle.astype(f32)).astype(bf16)
    split = jnp.concatenate(
        [high, middle, low, jnp.zeros((128 - 3 * slots, exact.shape[1]), bf16)], axis=0
    )
    step = 2 * width
    for n in range(0, 16 * width, step):
        picked[:, n : n + step] = jnp.dot(pick, split[:, n : n + step], preferred_element_type=f32)

    out_row = lax.broadcasted_iota(jnp.int32, (size, size), 0)
    in_row = lax.broadcasted_iota(jnp.int32, (size, size), 1)
    wanted = (out_row % group) * 8 + out_row // group
    shuffle = jnp.where(in_row == wanted, 1.0, 0.0).astype(bf16)
    for g in range(rows // group):
        part = jnp.dot(
            shuffle, model_ref[g * size : (g + 1) * size, :], preferred_element_type=f32
        )
        for j in range(8):
            model_parts[j, g * group : (g + 1) * group, :] = part[j * group : (j + 1) * group, :]

    def chunk(i, carry):
        at = pl.ds(pl.multiple_of(i * 8, 8), 8)
        at_q = pl.ds(pl.multiple_of(rows + i * 8, 8), 8)
        cols = [slice(j * width, (j + 1) * width) for j in range(16)]
        model = [model_parts[j, at, :] for j in range(8)]
        right = times_adjoint(model, [picked[at_q, c] for c in cols[:8]])
        left = times([picked[at, c] for c in cols[:8]], model)
        one = times([picked[at, c] for c in cols[8:]], right)
        two = times_adjoint(left, [picked[at_q, c] for c in cols[8:]])
        change = [a + b for a, b in zip(one, two)]
        for c, value in zip(cols, times_adjoint(change, right)):
            grads[at, c] = value
        for c, value in zip(cols, adjoint_times(change, left)):
            grads[at_q, c] = value
        return carry

    lax.fori_loop(0, rows // 8, chunk, 0, unroll=2)
    sums = []
    for n in range(0, 8 * width, step):
        value = grads[:, n : n + step]
        high = value.astype(bf16)
        low = (value - high.astype(f32)).astype(bf16)
        total = jnp.dot(scatter, high, preferred_element_type=f32) + jnp.dot(
            scatter, low, preferred_element_type=f32
        )
        table[:, n : n + step] = factor * total
    for k, ref in enumerate((own_out, even_out, odd_out, far_out)):
        for j in range(8):
            ref[j * owned : (j + 1) * owned, :] = table[
                k * owned : (k + 1) * owned, j * width : (j + 1) * width
            ]


def curvature_kernel(
    own_ref, even_ref, odd_ref, far_ref, terms_ref, turn_ref, small_ref, band_ref, res_ref,
    curv_ref, row_ref, *, channels
):
    owned, _, width = band_ref.shape
    half = 2 * owned
    delay_scale = channels ** (-0.5)
    freq = frequencies(chan_index(), width, channels)
    cosine = turn_ref[0:half, :]
    sine = turn_ref[half : 2 * half, :]
    total = own_ref[...] + even_ref[...] + odd_ref[lax.axis_index("base") % 2] + far_ref[...]
    moved = jnp.zeros((half, width), f32)
    for r in range(2):
        re = slice(r * half, (r + 1) * half)
        im = slice((2 + r) * half, (3 + r) * half)
        grad_re, grad_im = total[re, :], total[im, :]
        moved = moved + (terms_ref[re, :] * grad_im - terms_ref[im, :] * grad_re)
        band_re = cosine * grad_re + sine * grad_im
        band_im = cosine * grad_im - sine * grad_re
        for a in range(2):
            rows = slice(a * owned, (a + 1) * owned)
            j = 2 * r + a
            curv_ref[:, j, :] = band_re[rows, :] + damping_weight * band_ref[:, j, :]
            curv_ref[:, 4 + j, :] = band_im[rows, :] + damping_weight * band_ref[:, 4 + j, :]
    moved = jnp.sum(moved * (full_turn * delay_scale * freq), axis=1, keepdims=True)
    curv, band, res = curv_ref[...], band_ref[...], res_ref[...]
    scalars = [
        jnp.sum(jnp.sum(jnp.sum(x, axis=0), axis=0, keepdims=True), axis=1, keepdims=True)
        for x in (res * res, res * curv, curv * curv, band * curv)
    ]
    here = jnp.where(lax.axis_index("z") == 0, 1.0, 0.0)
    values = jnp.concatenate(
        [moved] + scalars + [jnp.zeros((4, 1), f32)]
        + [here * column(small_ref.at[0]), here * column(small_ref.at[1])],
        axis=0,
    )
    count = values.shape[0]
    diagonal = lax.broadcasted_iota(jnp.int32, (count, width), 0) == lax.broadcasted_iota(
        jnp.int32, (count, width), 1
    )
    row = jnp.sum(
        jnp.where(diagonal, jnp.broadcast_to(values, (count, width)), 0.0), axis=0, keepdims=True
    )
    row_ref[...] = jnp.broadcast_to(row, row_ref.shape)


def update_kernel(
    rows_ref, curv_ref, small_ref, band_ref, res_ref, iter_ref,
    iter_out, iter_delay_out, res_out, res_delay_out, dir_out, dir_delay_out
):
    rows = rows_ref[...]
    count, width = rows.shape
    owned = band_ref.shape[0]
    half = 2 * owned
    sums = jnp.sum(rows, axis=0, keepdims=True)
    lane = lax.broadcasted_iota(jnp.int32, (1, width), 1)

    def scalar(x):
        return jnp.sum(x, axis=1, keepdims=True)

    pair = rows + pltpu.roll(rows, count - 1, 0)
    moves = pltpu.roll(rows, width - 16, 1)
    lefts = pltpu.roll(rows, width - 24, 1)
    curves = pair + damping_weight * moves
    valid = (lax.broadcasted_iota(jnp.int32, (count, width), 0) % 2 == 0) & (
        lax.broadcasted_iota(jnp.int32, (count, width), 1) < half
    )

    def delays(x):
        return scalar(jnp.sum(jnp.where(valid, x, 0.0), axis=0, keepdims=True))

    squares = scalar(jnp.where(lane == half, sums, 0.0)) + delays(lefts * lefts)
    cross = scalar(jnp.where(lane == half + 1, sums, 0.0)) + delays(lefts * curves)
    norm = scalar(jnp.where(lane == half + 2, sums, 0.0)) + delays(curves * curves)
    curvature = scalar(jnp.where(lane == half + 3, sums, 0.0)) + delays(moves * curves)
    alpha = squares / curvature
    fresh = squares + alpha * (alpha * norm - 2.0 * cross)
    ratio = fresh / squares

    band, curv = band_ref[...], curv_ref[...]
    alpha3 = alpha.reshape(1, 1, 1)
    ratio3 = ratio.reshape(1, 1, 1)
    iter_out[...] = iter_ref[...] + alpha3 * band
    new_res = res_ref[...] - alpha3 * curv
    res_out[...] = new_res
    dir_out[...] = new_res + ratio3 * band

    mine = lax.broadcasted_iota(jnp.int32, (count, width), 0) == 2 * lax.axis_index("base")
    own = jnp.sum(jnp.where(mine, pair, 0.0), axis=0, keepdims=True)
    own = jnp.concatenate([own[:, 0:owned], own[:, owned:half]], axis=0)
    move = small_ref[0]
    iter_delay_out[...] = small_ref[2] + alpha * move
    new_left = small_ref[1] - alpha * (own + damping_weight * move)
    res_delay_out[...] = new_left
    dir_delay_out[...] = new_left + ratio * move


def body(
    gains,
    delays,
    model,
    antenna1,
    antenna2,
    dir_band,
    dir_delay,
    res_band,
    res_delay,
    iter_band,
    iter_delay,
):
    owned, _, width = gains.shape
    rows = model.shape[0]
    blocks = lax.axis_size("base")
    lines = lax.axis_size("z")
    cores = lax.axis_size("core")
    channels = width * lines * cores
    slots = 4 * owned
    factor = owned / (2.0 * rows)
    delays_t, dir_delay_t, res_delay_t, iter_delay_t = (
        jnp.transpose(x) for x in (delays, dir_delay, res_delay, iter_delay)
    )

    terms, turn, small, gather, scatter, model_local = pl.pallas_call(
        lambda *refs: station_kernel(*refs, channels=channels, blocks=blocks),
        out_shape=(
            shape(16 * owned, width),
            shape(4 * owned, width),
            shape(3, 2, owned),
            shape(2 * rows, 128, dtype=bf16),
            shape(slots, 2 * rows, dtype=bf16),
            shape(8 * rows, width, dtype=bf16),
        ),
        in_specs=[hbm()] * 9,
        out_specs=(vmem(),) * 6,
        scratch_shapes=[
            pltpu.VMEM((owned, 8, width), f32),
            pltpu.VMEM((owned, 8, width), f32),
            pltpu.VMEM((2, owned), f32),
            pltpu.VMEM((2, rows), jnp.int32),
            pltpu.VMEM((16 * owned, width), f32),
            pltpu.SemaphoreType.DMA((9,)),
        ],
        compiler_params=params(4),
        name="station_terms",
    )(
        *(
            pltpu.with_memory_space_constraint(x, pltpu.HBM)
            for x in (
                gains, dir_band, delays_t, dir_delay_t, res_delay_t, iter_delay_t,
                antenna1.reshape(1, rows), antenna2.reshape(1, rows), model.reshape(rows * 8, width),
            )
        )
    )

    far_pairs = [(i, (i + blocks // 2) % blocks) for i in range(blocks)]
    even_pairs = [(i, i ^ 1) for i in range(blocks)]
    odd_groups = [[i, (i + 1) % blocks] for i in range(1, blocks, 2)]

    def exchange(to_even, to_odd, to_far):
        far = lax.ppermute(to_far, "base", far_pairs)
        even = lax.ppermute(to_even, "base", even_pairs)
        odd = lax.all_gather(to_odd, "base", axis_index_groups=odd_groups)
        return even, odd, far

    own, to_even, to_odd, to_far = pl.pallas_call(
        lambda *refs: baseline_kernel(*refs, factor=factor),
        out_shape=(shape(8 * owned, width),) * 4,
        in_specs=[vmem()] * 7,
        out_specs=(vmem(),) * 4,
        scratch_shapes=[
            pltpu.VMEM((slots, 16 * width), f32),
            pltpu.VMEM((2 * rows, 16 * width), f32),
            pltpu.VMEM((2 * rows, 8 * width), f32),
            pltpu.VMEM((8, rows, width), f32),
        ],
        compiler_params=params(24),
        name="baselines",
    )(
        terms, *exchange(terms, terms, terms),
        model_local, gather, scatter,
    )

    curv, row = pl.pallas_call(
        lambda *refs: curvature_kernel(*refs, channels=channels),
        out_shape=(shape(owned, 8, width), shape(lines, width)),
        in_specs=[vmem()] * 9,
        out_specs=(vmem(), vmem()),
        compiler_params=params(4),
        name="curvature",
    )(own, *exchange(to_even, to_odd, to_far), terms, turn, small, dir_band, res_band)

    line = lax.all_to_all(row, "z", 0, 0, tiled=True)
    peers = blocks * cores
    line = jnp.broadcast_to(jnp.sum(line, axis=0, keepdims=True), (peers, width))
    everyone = lax.all_to_all(line, ("base", "core"), 0, 0, tiled=True)

    outs = pl.pallas_call(
        update_kernel,
        out_shape=(
            shape(owned, 8, width),
            shape(2, owned),
            shape(owned, 8, width),
            shape(2, owned),
            shape(owned, 8, width),
            shape(2, owned),
        ),
        in_specs=[vmem()] * 6,
        out_specs=(vmem(),) * 6,
        compiler_params=params(4),
        name="update",
    )(everyone, curv, small, dir_band, res_band, iter_band)
    return (
        outs[0],
        jnp.transpose(outs[1]),
        outs[2],
        jnp.transpose(outs[3]),
        outs[4],
        jnp.transpose(outs[5]),
    )


def solution(mesh):
    cores = 2
    blocks, chans = mesh.shape["base"], mesh.shape["chan"]
    split = Mesh(mesh.devices.reshape(blocks, chans // cores, cores), ("base", "z", "core"))
    band = P("base", None, ("z", "core"))
    delay = P("base", None)
    one = P("base")
    return jax.shard_map(
        body,
        mesh=split,
        in_specs=(band, delay, band, one, one, band, delay, band, delay, band, delay),
        out_specs=(band, delay) * 3,
        check_vma=False,
    )
```

```python
import math

import jax
import jax.numpy as jnp
from jax import lax
from jax.experimental import pallas as pl
from jax.experimental.pallas import tpu as pltpu
from jax.sharding import Mesh
from jax.sharding import PartitionSpec as P

full_turn = 2.0 * math.pi
damping_weight = 0.5

f32 = jnp.float32
bf16 = jnp.bfloat16


def vmem():
    return pl.BlockSpec(memory_space=pltpu.VMEM)


def hbm():
    return pl.BlockSpec(memory_space=pltpu.HBM)


def params(mib):
    return pltpu.CompilerParams(vmem_limit_bytes=int(mib * 1024 * 1024))


def shape(*dims, dtype=f32):
    return jax.ShapeDtypeStruct(dims, dtype)


def chan_index():
    return lax.axis_index("z") * lax.axis_size("core") + lax.axis_index("core")


def frequencies(chan, width, channels):
    index = lax.broadcasted_iota(jnp.int32, (1, width), 1) + chan * width
    return (index.astype(f32) + 0.5) / channels - 0.5


def column(row_ref):
    count = row_ref.shape[1]
    eye = lax.broadcasted_iota(jnp.int32, (count, count), 0) == lax.broadcasted_iota(
        jnp.int32, (count, count), 1
    )
    parts = [
        jnp.sum(
            jnp.where(eye, jnp.broadcast_to(row_ref[a : a + 1, :], (count, count)), 0.0),
            axis=1,
            keepdims=True,
        )
        for a in range(2)
    ]
    return jnp.concatenate(parts, axis=0)


def pick_stations(ids, gather_ref, scatter_ref, *, owned, blocks):
    rows = ids.shape[1]
    slots = 4 * owned
    slot = lax.broadcasted_iota(jnp.int32, (slots, 2 * rows), 0)
    kind = slot // owned
    block = lax.axis_index("base")
    turn_up = 1 - 2 * (block % 2)
    offset = jnp.where(kind == 0, 0, jnp.where(kind == 1, turn_up, jnp.where(kind == 2, -turn_up, blocks // 2)))
    station = ((block + offset + blocks) % blocks) * owned + slot % owned
    both = jnp.concatenate([ids[0:1, :], ids[1:2, :]], axis=1)
    pick = jnp.where(station == both, 1.0, 0.0)
    filled = jnp.concatenate([pick] * 3 + [jnp.zeros((128 - 3 * slots, 2 * rows), f32)], axis=0)
    scatter_ref[...] = pick.astype(bf16)
    gather_ref[...] = jnp.transpose(filled).astype(bf16)


def station_kernel(
    gains_hbm, band_hbm, delays_hbm, move_hbm, left_hbm, iter_hbm, first_hbm, second_hbm, model_hbm,
    terms_ref, turn_ref, small_ref, gather_ref, scatter_ref, model_ref,
    gains_ref, band_ref, delays_ref, ids, packed, sems, *, channels, blocks
):
    owned, _, width = gains_ref.shape
    rows = ids.shape[1]
    half = 2 * owned
    pairs = [
        (first_hbm, ids.at[0:1]),
        (second_hbm, ids.at[1:2]),
        (delays_hbm, delays_ref),
        (move_hbm, small_ref.at[0]),
        (gains_hbm, gains_ref),
        (band_hbm, band_ref),
    ]
    parts = 1
    share = 8 * rows // parts
    for k in range(parts):
        at = pl.ds(k * share, share)
        pairs.append((model_hbm.at[at], model_ref.at[at]))
    pairs += [(left_hbm, small_ref.at[1]), (iter_hbm, small_ref.at[2])]
    copies = [pltpu.make_async_copy(a, b, sems.at[k]) for k, (a, b) in enumerate(pairs)]
    for copy in copies:
        copy.start()
    copies[0].wait()
    copies[1].wait()
    pick_stations(ids, gather_ref, scatter_ref, owned=owned, blocks=blocks)
    copies[2].wait()
    copies[3].wait()
    delay_scale = channels ** (-0.5)
    freq = frequencies(chan_index(), width, channels)
    phase = full_turn * column(delays_ref) * freq
    rate = full_turn * delay_scale * column(small_ref.at[0]) * freq
    cosine = jnp.cos(phase)
    sine = jnp.sin(phase)
    turn_ref[0:half, :] = cosine
    turn_ref[half : 2 * half, :] = sine
    copies[4].wait()
    copies[5].wait()
    for j in range(8):
        packed[j * owned : (j + 1) * owned, :] = gains_ref[:, j, :]
        packed[(8 + j) * owned : (9 + j) * owned, :] = band_ref[:, j, :]
    for r in range(2):
        re = slice(r * half, (r + 1) * half)
        im = slice((2 + r) * half, (3 + r) * half)
        move_re = slice((4 + r) * half, (5 + r) * half)
        move_im = slice((6 + r) * half, (7 + r) * half)
        jones_re = cosine * packed[re, :] - sine * packed[im, :]
        jones_im = cosine * packed[im, :] + sine * packed[re, :]
        terms_ref[re, :] = jones_re
        terms_ref[im, :] = jones_im
        terms_ref[move_re, :] = (
            cosine * packed[move_re, :] - sine * packed[move_im, :] - rate * jones_im
        )
        terms_ref[move_im, :] = (
            cosine * packed[move_im, :] + sine * packed[move_re, :] + rate * jones_re
        )
    for copy in copies[6:]:
        copy.wait()


def times(a, b):
    out = []
    for r in range(2):
        for c in range(2):
            out.append(
                a[r * 2] * b[c] - a[4 + r * 2] * b[4 + c] + a[r * 2 + 1] * b[2 + c] - a[5 + r * 2] * b[6 + c]
            )
    for r in range(2):
        for c in range(2):
            out.append(
                a[r * 2] * b[4 + c] + a[4 + r * 2] * b[c] + a[r * 2 + 1] * b[6 + c] + a[5 + r * 2] * b[2 + c]
            )
    return out


def times_adjoint(a, b):
    out = []
    for r in range(2):
        for c in range(2):
            out.append(
                a[r * 2] * b[c * 2]
                + a[4 + r * 2] * b[4 + c * 2]
                + a[r * 2 + 1] * b[c * 2 + 1]
                + a[5 + r * 2] * b[5 + c * 2]
            )
    for r in range(2):
        for c in range(2):
            out.append(
                a[4 + r * 2] * b[c * 2]
                - a[r * 2] * b[4 + c * 2]
                + a[5 + r * 2] * b[c * 2 + 1]
                - a[r * 2 + 1] * b[5 + c * 2]
            )
    return out


def adjoint_times(a, b):
    out = []
    for r in range(2):
        for c in range(2):
            out.append(
                a[r] * b[c] + a[4 + r] * b[4 + c] + a[2 + r] * b[2 + c] + a[6 + r] * b[6 + c]
            )
    for r in range(2):
        for c in range(2):
            out.append(
                a[r] * b[4 + c] - a[4 + r] * b[c] + a[2 + r] * b[6 + c] - a[6 + r] * b[2 + c]
            )
    return out


def baseline_kernel(
    own_ref, even_ref, odd_ref, far_ref, model_ref, gather_ref, scatter_ref,
    own_out, far_out, even_out, odd_out, table, picked, grads, model_parts, *, factor
):
    _, rows, width = model_parts.shape
    slots = table.shape[0]
    owned = slots // 4
    group = 32
    size = 8 * group
    partner = even_ref.at[1 - lax.axis_index("base") % 2]
    for k, ref in enumerate((own_ref, partner, odd_ref, far_ref)):
        for j in range(16):
            table[k * owned : (k + 1) * owned, j * width : (j + 1) * width] = ref[
                j * owned : (j + 1) * owned, :
            ]
    exact = table[...]
    high = exact.astype(bf16)
    rest = exact - high.astype(f32)
    middle = rest.astype(bf16)
    low = (rest - middle.astype(f32)).astype(bf16)
    split = jnp.concatenate(
        [high, middle, low, jnp.zeros((128 - 3 * slots, exact.shape[1]), bf16)], axis=0
    )
    out_row = lax.broadcasted_iota(jnp.int32, (size, size), 0)
    in_row = lax.broadcasted_iota(jnp.int32, (size, size), 1)
    wanted = (out_row % group) * 8 + out_row // group
    shuffle = jnp.where(in_row == wanted, 1.0, 0.0).astype(bf16)
    step = 2 * width
    cols = [slice(j * width, (j + 1) * width) for j in range(16)]
    stage = rows // 2
    def load(first):
        for g in range(first // group, (first + stage) // group):
            part = jnp.dot(
                shuffle, model_ref[g * size : (g + 1) * size, :], preferred_element_type=f32
            )
            for j in range(8):
                model_parts[j, g * group : (g + 1) * group, :] = part[j * group : (j + 1) * group, :]
        for base in (first, rows + first):
            pick = gather_ref[base : base + stage, :]
            for n in range(0, 16 * width, step):
                picked[base : base + stage, n : n + step] = jnp.dot(pick, split[:, n : n + step], preferred_element_type=f32)

    def chunk(i):
        at = slice(i * 8, i * 8 + 8)
        at_q = slice(rows + i * 8, rows + i * 8 + 8)
        model = [model_parts[j, at, :] for j in range(8)]
        right = times_adjoint(model, [picked[at_q, c] for c in cols[:8]])
        left = times([picked[at, c] for c in cols[:8]], model)
        one = times([picked[at, c] for c in cols[8:]], right)
        two = times_adjoint(left, [picked[at_q, c] for c in cols[8:]])
        change = [a + b for a, b in zip(one, two)]
        for c, value in zip(cols, times_adjoint(change, right)):
            grads[at, c] = value
        for c, value in zip(cols, adjoint_times(change, left)):
            grads[at_q, c] = value

    def collect(first):
        for n in range(0, 8 * width, step):
            total = None
            for base in (first, rows + first):
                value = grads[base : base + stage, n : n + step]
                sel = scatter_ref[:, base : base + stage]
                high = value.astype(bf16)
                low = (value - high.astype(f32)).astype(bf16)
                part = jnp.dot(sel, high, preferred_element_type=f32) + jnp.dot(
                    sel, low, preferred_element_type=f32
                )
                total = part if total is None else total + part
            if first:
                table[:, n : n + step] = table[:, n : n + step] + factor * total
            else:
                table[:, n : n + step] = factor * total

    load(0)
    for first in range(0, rows, stage):
        if first + stage < rows:
            load(first + stage)
        for i in range(first // 8, (first + stage) // 8):
            chunk(i)
        collect(first)
    for k, ref in enumerate((own_out, even_out, odd_out, far_out)):
        for j in range(8):
            ref[j * owned : (j + 1) * owned, :] = table[
                k * owned : (k + 1) * owned, j * width : (j + 1) * width
            ]


def curvature_kernel(
    own_ref, far_ref, even_ref, odd_ref, terms_ref, turn_ref, small_ref, band_ref, res_ref,
    curv_ref, row_ref, *, channels
):
    owned, _, width = band_ref.shape
    half = 2 * owned
    delay_scale = channels ** (-0.5)
    freq = frequencies(chan_index(), width, channels)
    cosine = turn_ref[0:half, :]
    sine = turn_ref[half : 2 * half, :]
    total = own_ref[...] + even_ref[1 - lax.axis_index("base") % 2] + odd_ref[...] + far_ref[...]
    moved = jnp.zeros((half, width), f32)
    for r in range(2):
        re = slice(r * half, (r + 1) * half)
        im = slice((2 + r) * half, (3 + r) * half)
        grad_re, grad_im = total[re, :], total[im, :]
        moved = moved + (terms_ref[re, :] * grad_im - terms_ref[im, :] * grad_re)
        band_re = cosine * grad_re + sine * grad_im
        band_im = cosine * grad_im - sine * grad_re
        for a in range(2):
            rows = slice(a * owned, (a + 1) * owned)
            j = 2 * r + a
            curv_ref[:, j, :] = band_re[rows, :] + damping_weight * band_ref[:, j, :]
            curv_ref[:, 4 + j, :] = band_im[rows, :] + damping_weight * band_ref[:, 4 + j, :]
    moved = jnp.sum(moved * (full_turn * delay_scale * freq), axis=1, keepdims=True)
    curv, band, res = curv_ref[...], band_ref[...], res_ref[...]
    scalars = [
        jnp.sum(jnp.sum(jnp.sum(x, axis=0), axis=0, keepdims=True), axis=1, keepdims=True)
        for x in (res * res, res * curv, curv * curv, band * curv)
    ]
    here = jnp.where(lax.axis_index("z") == 0, 1.0, 0.0)
    values = jnp.concatenate(
        [moved] + scalars + [jnp.zeros((4, 1), f32)]
        + [here * column(small_ref.at[0]), here * column(small_ref.at[1])],
        axis=0,
    )
    count = values.shape[0]
    diagonal = lax.broadcasted_iota(jnp.int32, (count, width), 0) == lax.broadcasted_iota(
        jnp.int32, (count, width), 1
    )
    row = jnp.sum(
        jnp.where(diagonal, jnp.broadcast_to(values, (count, width)), 0.0), axis=0, keepdims=True
    )
    row_ref[...] = jnp.broadcast_to(row, row_ref.shape)


def update_kernel(
    rows_ref, curv_ref, small_ref, band_ref, res_ref, iter_ref,
    iter_out, iter_delay_out, res_out, res_delay_out, dir_out, dir_delay_out
):
    rows = rows_ref[...]
    count, width = rows.shape
    owned = band_ref.shape[0]
    half = 2 * owned
    sums = jnp.sum(rows, axis=0, keepdims=True)
    lane = lax.broadcasted_iota(jnp.int32, (1, width), 1)

    def scalar(x):
        return jnp.sum(x, axis=1, keepdims=True)

    pair = rows + pltpu.roll(rows, count - 1, 0)
    moves = pltpu.roll(rows, width - 16, 1)
    lefts = pltpu.roll(rows, width - 24, 1)
    curves = pair + damping_weight * moves
    valid = (lax.broadcasted_iota(jnp.int32, (count, width), 0) % 2 == 0) & (
        lax.broadcasted_iota(jnp.int32, (count, width), 1) < half
    )

    def delays(x):
        return scalar(jnp.sum(jnp.where(valid, x, 0.0), axis=0, keepdims=True))

    squares = scalar(jnp.where(lane == half, sums, 0.0)) + delays(lefts * lefts)
    cross = scalar(jnp.where(lane == half + 1, sums, 0.0)) + delays(lefts * curves)
    norm = scalar(jnp.where(lane == half + 2, sums, 0.0)) + delays(curves * curves)
    curvature = scalar(jnp.where(lane == half + 3, sums, 0.0)) + delays(moves * curves)
    alpha = squares / curvature
    fresh = squares + alpha * (alpha * norm - 2.0 * cross)
    ratio = fresh / squares

    band, curv = band_ref[...], curv_ref[...]
    alpha3 = alpha.reshape(1, 1, 1)
    ratio3 = ratio.reshape(1, 1, 1)
    iter_out[...] = iter_ref[...] + alpha3 * band
    new_res = res_ref[...] - alpha3 * curv
    res_out[...] = new_res
    dir_out[...] = new_res + ratio3 * band

    mine = lax.broadcasted_iota(jnp.int32, (count, width), 0) == 2 * lax.axis_index("base")
    own = jnp.sum(jnp.where(mine, pair, 0.0), axis=0, keepdims=True)
    own = jnp.concatenate([own[:, 0:owned], own[:, owned:half]], axis=0)
    move = small_ref[0]
    iter_delay_out[...] = small_ref[2] + alpha * move
    new_left = small_ref[1] - alpha * (own + damping_weight * move)
    res_delay_out[...] = new_left
    dir_delay_out[...] = new_left + ratio * move


def body(
    gains,
    delays,
    model,
    antenna1,
    antenna2,
    dir_band,
    dir_delay,
    res_band,
    res_delay,
    iter_band,
    iter_delay,
):
    owned, _, width = gains.shape
    rows = model.shape[0]
    blocks = lax.axis_size("base")
    lines = lax.axis_size("z")
    cores = lax.axis_size("core")
    channels = width * lines * cores
    slots = 4 * owned
    factor = owned / (2.0 * rows)
    delays_t, dir_delay_t, res_delay_t, iter_delay_t = (
        jnp.transpose(x) for x in (delays, dir_delay, res_delay, iter_delay)
    )

    terms, turn, small, gather, scatter, model_local = pl.pallas_call(
        lambda *refs: station_kernel(*refs, channels=channels, blocks=blocks),
        out_shape=(
            shape(16 * owned, width),
            shape(4 * owned, width),
            shape(3, 2, owned),
            shape(2 * rows, 128, dtype=bf16),
            shape(slots, 2 * rows, dtype=bf16),
            shape(8 * rows, width, dtype=bf16),
        ),
        in_specs=[hbm()] * 9,
        out_specs=(vmem(),) * 6,
        scratch_shapes=[
            pltpu.VMEM((owned, 8, width), f32),
            pltpu.VMEM((owned, 8, width), f32),
            pltpu.VMEM((2, owned), f32),
            pltpu.VMEM((2, rows), jnp.int32),
            pltpu.VMEM((16 * owned, width), f32),
            pltpu.SemaphoreType.DMA((9,)),
        ],
        compiler_params=params(4),
        name="station_terms",
    )(
        *(
            pltpu.with_memory_space_constraint(x, pltpu.HBM)
            for x in (
                gains, dir_band, delays_t, dir_delay_t, res_delay_t, iter_delay_t,
                antenna1.reshape(1, rows), antenna2.reshape(1, rows), model.reshape(rows * 8, width),
            )
        )
    )

    far_pairs = [(i, (i + blocks // 2) % blocks) for i in range(blocks)]
    odd_pairs = [(i, (i + 1) % blocks if i % 2 else (i - 1) % blocks) for i in range(blocks)]
    even_groups = [[i, i + 1] for i in range(0, blocks, 2)]

    def exchange(to_even, to_odd, to_far):
        far = lax.ppermute(to_far, "base", far_pairs)
        odd = lax.ppermute(to_odd, "base", odd_pairs)
        even = lax.all_gather(to_even, "base", axis_index_groups=even_groups)
        return even, odd, far

    own, to_far, to_even, to_odd = pl.pallas_call(
        lambda *refs: baseline_kernel(*refs, factor=factor),
        out_shape=(shape(8 * owned, width),) * 4,
        in_specs=[vmem()] * 7,
        out_specs=(vmem(),) * 4,
        scratch_shapes=[
            pltpu.VMEM((slots, 16 * width), f32),
            pltpu.VMEM((2 * rows, 16 * width), f32),
            pltpu.VMEM((2 * rows, 8 * width), f32),
            pltpu.VMEM((8, rows, width), f32),
        ],
        compiler_params=params(24),
        name="baselines",
    )(
        terms, *exchange(terms, terms, terms),
        model_local, gather, scatter,
    )

    from_even, from_odd, from_far = exchange(to_even, to_odd, to_far)
    curv, row = pl.pallas_call(
        lambda *refs: curvature_kernel(*refs, channels=channels),
        out_shape=(shape(owned, 8, width), shape(lines, width)),
        in_specs=[vmem()] * 9,
        out_specs=(vmem(), vmem()),
        compiler_params=params(4),
        name="curvature",
    )(own, from_far, from_even, from_odd, terms, turn, small, dir_band, res_band)

    line = lax.all_to_all(row, "z", 0, 0, tiled=True)
    peers = blocks * cores
    line = jnp.broadcast_to(jnp.sum(line, axis=0, keepdims=True), (peers, width))
    everyone = lax.all_to_all(line, ("base", "core"), 0, 0, tiled=True)

    outs = pl.pallas_call(
        update_kernel,
        out_shape=(
            shape(owned, 8, width),
            shape(2, owned),
            shape(owned, 8, width),
            shape(2, owned),
            shape(owned, 8, width),
            shape(2, owned),
        ),
        in_specs=[vmem()] * 6,
        out_specs=(vmem(),) * 6,
        compiler_params=params(4),
        name="update",
    )(everyone, curv, small, dir_band, res_band, iter_band)
    return (
        outs[0],
        jnp.transpose(outs[1]),
        outs[2],
        jnp.transpose(outs[3]),
        outs[4],
        jnp.transpose(outs[5]),
    )


def solution(mesh):
    cores = 2
    blocks, chans = mesh.shape["base"], mesh.shape["chan"]
    split = Mesh(mesh.devices.reshape(blocks, chans // cores, cores), ("base", "z", "core"))
    band = P("base", None, ("z", "core"))
    delay = P("base", None)
    one = P("base")
    return jax.shard_map(
        body,
        mesh=split,
        in_specs=(band, delay, band, one, one, band, delay, band, delay, band, delay),
        out_specs=(band, delay) * 3,
        check_vma=False,
    )
```

```python
import math

import jax
import jax.numpy as jnp
from jax import lax
from jax.experimental import pallas as pl
from jax.experimental.pallas import tpu as pltpu
from jax.sharding import Mesh
from jax.sharding import PartitionSpec as P

full_turn = 2.0 * math.pi
damping_weight = 0.5

f32 = jnp.float32
bf16 = jnp.bfloat16


def vmem():
    return pl.BlockSpec(memory_space=pltpu.VMEM)


def hbm():
    return pl.BlockSpec(memory_space=pltpu.HBM)


def params(mib):
    return pltpu.CompilerParams(vmem_limit_bytes=int(mib * 1024 * 1024))


def shape(*dims, dtype=f32):
    return jax.ShapeDtypeStruct(dims, dtype)


def group_place(blocks):
    block = lax.axis_index("base")
    first = jnp.where(block % 2 == 1, block, (block + blocks - 1) % blocks)
    return 1 - block % 2 + 2 * jnp.where(first >= blocks // 2, 1, 0)


def chan_index():
    return lax.axis_index("z") * lax.axis_size("core") + lax.axis_index("core")


def frequencies(chan, width, channels):
    index = lax.broadcasted_iota(jnp.int32, (1, width), 1) + chan * width
    return (index.astype(f32) + 0.5) / channels - 0.5


def column(row_ref):
    count = row_ref.shape[1]
    eye = lax.broadcasted_iota(jnp.int32, (count, count), 0) == lax.broadcasted_iota(
        jnp.int32, (count, count), 1
    )
    parts = [
        jnp.sum(
            jnp.where(eye, jnp.broadcast_to(row_ref[a : a + 1, :], (count, count)), 0.0),
            axis=1,
            keepdims=True,
        )
        for a in range(2)
    ]
    return jnp.concatenate(parts, axis=0)


def pick_stations(ids, gather_ref, scatter_ref, *, owned, blocks):
    rows = ids.shape[1]
    slots = 4 * owned
    slot = lax.broadcasted_iota(jnp.int32, (slots, 2 * rows), 0)
    kind = slot // owned
    block = lax.axis_index("base")
    turn_up = 1 - 2 * (block % 2)
    offset = jnp.where(kind == 0, 0, jnp.where(kind == 1, turn_up, jnp.where(kind == 2, -turn_up, blocks // 2)))
    station = ((block + offset + blocks) % blocks) * owned + slot % owned
    both = jnp.concatenate([ids[0:1, :], ids[1:2, :]], axis=1)
    pick = jnp.where(station == both, 1.0, 0.0)
    filled = jnp.concatenate([pick] * 3 + [jnp.zeros((128 - 3 * slots, 2 * rows), f32)], axis=0)
    scatter_ref[...] = pick.astype(bf16)
    gather_ref[...] = jnp.transpose(filled).astype(bf16)


def station_kernel(
    gains_hbm, band_hbm, delays_hbm, move_hbm, left_hbm, iter_hbm, first_hbm, second_hbm, model_hbm,
    terms_ref, turn_ref, small_ref, gather_ref, scatter_ref, model_ref,
    gains_ref, band_ref, delays_ref, ids, packed, sems, *, channels, blocks
):
    owned, _, width = gains_ref.shape
    rows = ids.shape[1]
    half = 2 * owned
    pairs = [
        (first_hbm, ids.at[0:1]),
        (second_hbm, ids.at[1:2]),
        (delays_hbm, delays_ref),
        (move_hbm, small_ref.at[0]),
        (gains_hbm, gains_ref),
        (band_hbm, band_ref),
    ]
    parts = 1
    share = 8 * rows // parts
    for k in range(parts):
        at = pl.ds(k * share, share)
        pairs.append((model_hbm.at[at], model_ref.at[at]))
    pairs += [(left_hbm, small_ref.at[1]), (iter_hbm, small_ref.at[2])]
    copies = [pltpu.make_async_copy(a, b, sems.at[k]) for k, (a, b) in enumerate(pairs)]
    for copy in copies:
        copy.start()
    copies[0].wait()
    copies[1].wait()
    pick_stations(ids, gather_ref, scatter_ref, owned=owned, blocks=blocks)
    copies[2].wait()
    copies[3].wait()
    delay_scale = channels ** (-0.5)
    freq = frequencies(chan_index(), width, channels)
    phase = full_turn * column(delays_ref) * freq
    rate = full_turn * delay_scale * column(small_ref.at[0]) * freq
    cosine = jnp.cos(phase)
    sine = jnp.sin(phase)
    turn_ref[0:half, :] = cosine
    turn_ref[half : 2 * half, :] = sine
    copies[4].wait()
    copies[5].wait()
    for j in range(8):
        packed[j * owned : (j + 1) * owned, :] = gains_ref[:, j, :]
        packed[(8 + j) * owned : (9 + j) * owned, :] = band_ref[:, j, :]
    for r in range(2):
        re = slice(r * half, (r + 1) * half)
        im = slice((2 + r) * half, (3 + r) * half)
        move_re = slice((4 + r) * half, (5 + r) * half)
        move_im = slice((6 + r) * half, (7 + r) * half)
        jones_re = cosine * packed[re, :] - sine * packed[im, :]
        jones_im = cosine * packed[im, :] + sine * packed[re, :]
        terms_ref[re, :] = jones_re
        terms_ref[im, :] = jones_im
        terms_ref[move_re, :] = (
            cosine * packed[move_re, :] - sine * packed[move_im, :] - rate * jones_im
        )
        terms_ref[move_im, :] = (
            cosine * packed[move_im, :] + sine * packed[move_re, :] + rate * jones_re
        )
    for copy in copies[6:]:
        copy.wait()


def times(a, b):
    out = []
    for r in range(2):
        for c in range(2):
            out.append(
                a[r * 2] * b[c] - a[4 + r * 2] * b[4 + c] + a[r * 2 + 1] * b[2 + c] - a[5 + r * 2] * b[6 + c]
            )
    for r in range(2):
        for c in range(2):
            out.append(
                a[r * 2] * b[4 + c] + a[4 + r * 2] * b[c] + a[r * 2 + 1] * b[6 + c] + a[5 + r * 2] * b[2 + c]
            )
    return out


def times_adjoint(a, b):
    out = []
    for r in range(2):
        for c in range(2):
            out.append(
                a[r * 2] * b[c * 2]
                + a[4 + r * 2] * b[4 + c * 2]
                + a[r * 2 + 1] * b[c * 2 + 1]
                + a[5 + r * 2] * b[5 + c * 2]
            )
    for r in range(2):
        for c in range(2):
            out.append(
                a[4 + r * 2] * b[c * 2]
                - a[r * 2] * b[4 + c * 2]
                + a[5 + r * 2] * b[c * 2 + 1]
                - a[r * 2 + 1] * b[5 + c * 2]
            )
    return out


def adjoint_times(a, b):
    out = []
    for r in range(2):
        for c in range(2):
            out.append(
                a[r] * b[c] + a[4 + r] * b[4 + c] + a[2 + r] * b[2 + c] + a[6 + r] * b[6 + c]
            )
    for r in range(2):
        for c in range(2):
            out.append(
                a[r] * b[4 + c] - a[4 + r] * b[c] + a[2 + r] * b[6 + c] - a[6 + r] * b[2 + c]
            )
    return out


def baseline_kernel(
    own_ref, even_ref, odd_ref, far_ref, model_ref, gather_ref, scatter_ref,
    even_out, group_out, table, picked, grads, model_parts, *, factor, blocks
):
    _, rows, width = model_parts.shape
    slots = table.shape[0]
    owned = slots // 4
    group = 32
    size = 8 * group
    place = group_place(blocks)
    odd_place = place + 1 - 2 * (place % 2)
    far_place = (place + 2) % 4
    partner = even_ref.at[1 - lax.axis_index("base") % 2]
    sources = (own_ref, partner, odd_ref, far_ref)
    for k, ref in enumerate(sources):
        for j in range(16):
            table[k * owned : (k + 1) * owned, j * width : (j + 1) * width] = ref[
                j * owned : (j + 1) * owned, :
            ]
    exact = table[...]
    high = exact.astype(bf16)
    rest = exact - high.astype(f32)
    middle = rest.astype(bf16)
    low = (rest - middle.astype(f32)).astype(bf16)
    split = jnp.concatenate(
        [high, middle, low, jnp.zeros((128 - 3 * slots, exact.shape[1]), bf16)], axis=0
    )
    out_row = lax.broadcasted_iota(jnp.int32, (size, size), 0)
    in_row = lax.broadcasted_iota(jnp.int32, (size, size), 1)
    wanted = (out_row % group) * 8 + out_row // group
    shuffle = jnp.where(in_row == wanted, 1.0, 0.0).astype(bf16)
    step = 2 * width
    cols = [slice(j * width, (j + 1) * width) for j in range(16)]
    stage = rows // 2
    def load(first):
        for g in range(first // group, (first + stage) // group):
            part = jnp.dot(
                shuffle, model_ref[g * size : (g + 1) * size, :], preferred_element_type=f32
            )
            for j in range(8):
                model_parts[j, g * group : (g + 1) * group, :] = part[j * group : (j + 1) * group, :]
        for base in (first, rows + first):
            pick = gather_ref[base : base + stage, :]
            for n in range(0, 16 * width, step):
                picked[base : base + stage, n : n + step] = jnp.dot(pick, split[:, n : n + step], preferred_element_type=f32)

    def chunk(i):
        at = slice(i * 8, i * 8 + 8)
        at_q = slice(rows + i * 8, rows + i * 8 + 8)
        model = [model_parts[j, at, :] for j in range(8)]
        right = times_adjoint(model, [picked[at_q, c] for c in cols[:8]])
        left = times([picked[at, c] for c in cols[:8]], model)
        one = times([picked[at, c] for c in cols[8:]], right)
        two = times_adjoint(left, [picked[at_q, c] for c in cols[8:]])
        change = [a + b for a, b in zip(one, two)]
        for c, value in zip(cols, times_adjoint(change, right)):
            grads[at, c] = value
        for c, value in zip(cols, adjoint_times(change, left)):
            grads[at_q, c] = value

    def collect(first):
        for n in range(0, 8 * width, step):
            total = None
            for base in (first, rows + first):
                value = grads[base : base + stage, n : n + step]
                sel = scatter_ref[:, base : base + stage]
                high = value.astype(bf16)
                low = (value - high.astype(f32)).astype(bf16)
                part = jnp.dot(sel, high, preferred_element_type=f32) + jnp.dot(
                    sel, low, preferred_element_type=f32
                )
                total = part if total is None else total + part
            if first:
                table[:, n : n + step] = table[:, n : n + step] + factor * total
            else:
                table[:, n : n + step] = factor * total

    load(0)
    for first in range(0, rows, stage):
        if first + stage < rows:
            load(first + stage)
        for i in range(first // 8, (first + stage) // 8):
            chunk(i)
        collect(first)
    group_out[(odd_place + 2) % 4] = jnp.zeros(even_out.shape, f32)
    sinks = (group_out.at[place], even_out, group_out.at[odd_place], group_out.at[far_place])
    for k, ref in enumerate(sinks):
        for j in range(8):
            ref[j * owned : (j + 1) * owned, :] = table[
                k * owned : (k + 1) * owned, j * width : (j + 1) * width
            ]


def curvature_kernel(
    even_ref, group_ref, terms_ref, turn_ref, small_ref, band_ref, res_ref,
    curv_ref, row_ref, *, channels
):
    owned, _, width = band_ref.shape
    half = 2 * owned
    delay_scale = channels ** (-0.5)
    freq = frequencies(chan_index(), width, channels)
    cosine = turn_ref[0:half, :]
    sine = turn_ref[half : 2 * half, :]
    total = even_ref[1 - lax.axis_index("base") % 2]
    for k in range(4):
        total = total + group_ref[k]
    moved = jnp.zeros((half, width), f32)
    for r in range(2):
        re = slice(r * half, (r + 1) * half)
        im = slice((2 + r) * half, (3 + r) * half)
        grad_re, grad_im = total[re, :], total[im, :]
        moved = moved + (terms_ref[re, :] * grad_im - terms_ref[im, :] * grad_re)
        band_re = cosine * grad_re + sine * grad_im
        band_im = cosine * grad_im - sine * grad_re
        for a in range(2):
            rows = slice(a * owned, (a + 1) * owned)
            j = 2 * r + a
            curv_ref[:, j, :] = band_re[rows, :] + damping_weight * band_ref[:, j, :]
            curv_ref[:, 4 + j, :] = band_im[rows, :] + damping_weight * band_ref[:, 4 + j, :]
    moved = jnp.sum(moved * (full_turn * delay_scale * freq), axis=1, keepdims=True)
    curv, band, res = curv_ref[...], band_ref[...], res_ref[...]
    scalars = [
        jnp.sum(jnp.sum(jnp.sum(x, axis=0), axis=0, keepdims=True), axis=1, keepdims=True)
        for x in (res * res, res * curv, curv * curv, band * curv)
    ]
    here = jnp.where(lax.axis_index("z") == 0, 1.0, 0.0)
    values = jnp.concatenate(
        [moved] + scalars + [jnp.zeros((4, 1), f32)]
        + [here * column(small_ref.at[0]), here * column(small_ref.at[1])],
        axis=0,
    )
    count = values.shape[0]
    diagonal = lax.broadcasted_iota(jnp.int32, (count, width), 0) == lax.broadcasted_iota(
        jnp.int32, (count, width), 1
    )
    row = jnp.sum(
        jnp.where(diagonal, jnp.broadcast_to(values, (count, width)), 0.0), axis=0, keepdims=True
    )
    row_ref[...] = jnp.broadcast_to(row, row_ref.shape)


def update_kernel(
    rows_ref, curv_ref, small_ref, band_ref, res_ref, iter_ref,
    iter_out, iter_delay_out, res_out, res_delay_out, dir_out, dir_delay_out
):
    rows = rows_ref[...]
    count, width = rows.shape
    owned = band_ref.shape[0]
    half = 2 * owned
    sums = jnp.sum(rows, axis=0, keepdims=True)
    lane = lax.broadcasted_iota(jnp.int32, (1, width), 1)

    def scalar(x):
        return jnp.sum(x, axis=1, keepdims=True)

    pair = rows + pltpu.roll(rows, count - 1, 0)
    moves = pltpu.roll(rows, width - 16, 1)
    lefts = pltpu.roll(rows, width - 24, 1)
    curves = pair + damping_weight * moves
    valid = (lax.broadcasted_iota(jnp.int32, (count, width), 0) % 2 == 0) & (
        lax.broadcasted_iota(jnp.int32, (count, width), 1) < half
    )

    def delays(x):
        return scalar(jnp.sum(jnp.where(valid, x, 0.0), axis=0, keepdims=True))

    squares = scalar(jnp.where(lane == half, sums, 0.0)) + delays(lefts * lefts)
    cross = scalar(jnp.where(lane == half + 1, sums, 0.0)) + delays(lefts * curves)
    norm = scalar(jnp.where(lane == half + 2, sums, 0.0)) + delays(curves * curves)
    curvature = scalar(jnp.where(lane == half + 3, sums, 0.0)) + delays(moves * curves)
    alpha = squares / curvature
    fresh = squares + alpha * (alpha * norm - 2.0 * cross)
    ratio = fresh / squares

    band, curv = band_ref[...], curv_ref[...]
    alpha3 = alpha.reshape(1, 1, 1)
    ratio3 = ratio.reshape(1, 1, 1)
    iter_out[...] = iter_ref[...] + alpha3 * band
    new_res = res_ref[...] - alpha3 * curv
    res_out[...] = new_res
    dir_out[...] = new_res + ratio3 * band

    mine = lax.broadcasted_iota(jnp.int32, (count, width), 0) == 2 * lax.axis_index("base")
    own = jnp.sum(jnp.where(mine, pair, 0.0), axis=0, keepdims=True)
    own = jnp.concatenate([own[:, 0:owned], own[:, owned:half]], axis=0)
    move = small_ref[0]
    iter_delay_out[...] = small_ref[2] + alpha * move
    new_left = small_ref[1] - alpha * (own + damping_weight * move)
    res_delay_out[...] = new_left
    dir_delay_out[...] = new_left + ratio * move


def body(
    gains,
    delays,
    model,
    antenna1,
    antenna2,
    dir_band,
    dir_delay,
    res_band,
    res_delay,
    iter_band,
    iter_delay,
):
    owned, _, width = gains.shape
    rows = model.shape[0]
    blocks = lax.axis_size("base")
    lines = lax.axis_size("z")
    cores = lax.axis_size("core")
    channels = width * lines * cores
    slots = 4 * owned
    factor = owned / (2.0 * rows)
    delays_t, dir_delay_t, res_delay_t, iter_delay_t = (
        jnp.transpose(x) for x in (delays, dir_delay, res_delay, iter_delay)
    )

    terms, turn, small, gather, scatter, model_local = pl.pallas_call(
        lambda *refs: station_kernel(*refs, channels=channels, blocks=blocks),
        out_shape=(
            shape(16 * owned, width),
            shape(4 * owned, width),
            shape(3, 2, owned),
            shape(2 * rows, 128, dtype=bf16),
            shape(slots, 2 * rows, dtype=bf16),
            shape(8 * rows, width, dtype=bf16),
        ),
        in_specs=[hbm()] * 9,
        out_specs=(vmem(),) * 6,
        scratch_shapes=[
            pltpu.VMEM((owned, 8, width), f32),
            pltpu.VMEM((owned, 8, width), f32),
            pltpu.VMEM((2, owned), f32),
            pltpu.VMEM((2, rows), jnp.int32),
            pltpu.VMEM((16 * owned, width), f32),
            pltpu.SemaphoreType.DMA((9,)),
        ],
        compiler_params=params(4),
        name="station_terms",
    )(
        *(
            pltpu.with_memory_space_constraint(x, pltpu.HBM)
            for x in (
                gains, dir_band, delays_t, dir_delay_t, res_delay_t, iter_delay_t,
                antenna1.reshape(1, rows), antenna2.reshape(1, rows), model.reshape(rows * 8, width),
            )
        )
    )

    even_groups = [[i, i + 1] for i in range(0, blocks, 2)]
    half = blocks // 2
    groups = [[i, i + 1, i + half, (i + 1 + half) % blocks] for i in range(1, half, 2)]

    def exchange(to_even, to_group):
        count = to_group.shape[1]
        group = lax.all_to_all(
            to_group.reshape(4 * count, width), "base", 0, 0, axis_index_groups=groups, tiled=True
        )
        even = lax.all_gather(to_even, "base", axis_index_groups=even_groups)
        return even, group.reshape(4, count, width)

    far_pairs = [(i, (i + half) % blocks) for i in range(blocks)]
    odd_pairs = [(i, (i + 1) % blocks if i % 2 else (i - 1) % blocks) for i in range(blocks)]
    from_far = lax.ppermute(terms, "base", far_pairs)
    from_odd = lax.ppermute(terms, "base", odd_pairs)
    from_even = lax.all_gather(terms, "base", axis_index_groups=even_groups)

    to_even, to_group = pl.pallas_call(
        lambda *refs: baseline_kernel(*refs, factor=factor, blocks=blocks),
        out_shape=(shape(8 * owned, width), shape(4, 8 * owned, width)),
        in_specs=[vmem()] * 7,
        out_specs=(vmem(),) * 2,
        scratch_shapes=[
            pltpu.VMEM((slots, 16 * width), f32),
            pltpu.VMEM((2 * rows, 16 * width), f32),
            pltpu.VMEM((2 * rows, 8 * width), f32),
            pltpu.VMEM((8, rows, width), f32),
        ],
        compiler_params=params(24),
        name="baselines",
    )(terms, from_even, from_odd, from_far, model_local, gather, scatter)

    curv, row = pl.pallas_call(
        lambda *refs: curvature_kernel(*refs, channels=channels),
        out_shape=(shape(owned, 8, width), shape(lines, width)),
        in_specs=[vmem()] * 7,
        out_specs=(vmem(), vmem()),
        compiler_params=params(4),
        name="curvature",
    )(*exchange(to_even, to_group), terms, turn, small, dir_band, res_band)

    line = lax.all_to_all(row, "z", 0, 0, tiled=True)
    peers = blocks * cores
    line = jnp.broadcast_to(jnp.sum(line, axis=0, keepdims=True), (peers, width))
    everyone = lax.all_to_all(line, ("base", "core"), 0, 0, tiled=True)

    outs = pl.pallas_call(
        update_kernel,
        out_shape=(
            shape(owned, 8, width),
            shape(2, owned),
            shape(owned, 8, width),
            shape(2, owned),
            shape(owned, 8, width),
            shape(2, owned),
        ),
        in_specs=[vmem()] * 6,
        out_specs=(vmem(),) * 6,
        compiler_params=params(4),
        name="update",
    )(everyone, curv, small, dir_band, res_band, iter_band)
    return (
        outs[0],
        jnp.transpose(outs[1]),
        outs[2],
        jnp.transpose(outs[3]),
        outs[4],
        jnp.transpose(outs[5]),
    )


def solution(mesh):
    cores = 2
    blocks, chans = mesh.shape["base"], mesh.shape["chan"]
    split = Mesh(mesh.devices.reshape(blocks, chans // cores, cores), ("base", "z", "core"))
    band = P("base", None, ("z", "core"))
    delay = P("base", None)
    one = P("base")
    return jax.shard_map(
        body,
        mesh=split,
        in_specs=(band, delay, band, one, one, band, delay, band, delay, band, delay),
        out_specs=(band, delay) * 3,
        check_vma=False,
    )
```

```python
import math

import jax
import jax.numpy as jnp
from jax import lax
from jax.experimental import pallas as pl
from jax.experimental.pallas import tpu as pltpu
from jax.sharding import Mesh
from jax.sharding import PartitionSpec as P

full_turn = 2.0 * math.pi
damping_weight = 0.5

f32 = jnp.float32
bf16 = jnp.bfloat16


def vmem():
    return pl.BlockSpec(memory_space=pltpu.VMEM)


def hbm():
    return pl.BlockSpec(memory_space=pltpu.HBM)


def params(mib):
    return pltpu.CompilerParams(vmem_limit_bytes=int(mib * 1024 * 1024))


def shape(*dims, dtype=f32):
    return jax.ShapeDtypeStruct(dims, dtype)


def base_index():
    return lax.axis_index("y") * lax.axis_size("x") + lax.axis_index("x")


def group_place(blocks):
    block = base_index()
    first = jnp.where(block % 2 == 1, block, (block + blocks - 1) % blocks)
    return 1 - block % 2 + 2 * jnp.where(first >= blocks // 2, 1, 0)


def chan_index():
    return lax.axis_index("z") * lax.axis_size("core") + lax.axis_index("core")


def frequencies(chan, width, channels):
    index = lax.broadcasted_iota(jnp.int32, (1, width), 1) + chan * width
    return (index.astype(f32) + 0.5) / channels - 0.5


def column(row_ref):
    count = row_ref.shape[1]
    eye = lax.broadcasted_iota(jnp.int32, (count, count), 0) == lax.broadcasted_iota(
        jnp.int32, (count, count), 1
    )
    parts = [
        jnp.sum(
            jnp.where(eye, jnp.broadcast_to(row_ref[a : a + 1, :], (count, count)), 0.0),
            axis=1,
            keepdims=True,
        )
        for a in range(2)
    ]
    return jnp.concatenate(parts, axis=0)


def pick_stations(ids, gather_ref, scatter_ref, *, owned, blocks):
    rows = ids.shape[1]
    slots = 4 * owned
    slot = lax.broadcasted_iota(jnp.int32, (slots, 2 * rows), 0)
    kind = slot // owned
    block = base_index()
    turn_up = 1 - 2 * (block % 2)
    offset = jnp.where(kind == 0, 0, jnp.where(kind == 1, turn_up, jnp.where(kind == 2, -turn_up, blocks // 2)))
    station = ((block + offset + blocks) % blocks) * owned + slot % owned
    both = jnp.concatenate([ids[0:1, :], ids[1:2, :]], axis=1)
    pick = jnp.where(station == both, 1.0, 0.0)
    filled = jnp.concatenate([pick] * 3 + [jnp.zeros((128 - 3 * slots, 2 * rows), f32)], axis=0)
    scatter_ref[...] = pick.astype(bf16)
    gather_ref[...] = jnp.transpose(filled).astype(bf16)


def station_kernel(
    gains_hbm, band_hbm, delays_hbm, move_hbm, left_hbm, iter_hbm, first_hbm, second_hbm, model_hbm,
    terms_ref, turn_ref, small_ref, gather_ref, scatter_ref, model_ref,
    gains_ref, band_ref, delays_ref, ids, packed, sems, *, channels, blocks
):
    owned, _, width = gains_ref.shape
    rows = ids.shape[1]
    half = 2 * owned
    pairs = [
        (first_hbm, ids.at[0:1]),
        (second_hbm, ids.at[1:2]),
        (delays_hbm, delays_ref),
        (move_hbm, small_ref.at[0]),
        (gains_hbm, gains_ref),
        (band_hbm, band_ref),
    ]
    parts = 1
    share = 8 * rows // parts
    for k in range(parts):
        at = pl.ds(k * share, share)
        pairs.append((model_hbm.at[at], model_ref.at[at]))
    pairs += [(left_hbm, small_ref.at[1]), (iter_hbm, small_ref.at[2])]
    copies = [pltpu.make_async_copy(a, b, sems.at[k]) for k, (a, b) in enumerate(pairs)]
    for copy in copies:
        copy.start()
    copies[0].wait()
    copies[1].wait()
    pick_stations(ids, gather_ref, scatter_ref, owned=owned, blocks=blocks)
    copies[2].wait()
    copies[3].wait()
    delay_scale = channels ** (-0.5)
    freq = frequencies(chan_index(), width, channels)
    phase = full_turn * column(delays_ref) * freq
    rate = full_turn * delay_scale * column(small_ref.at[0]) * freq
    cosine = jnp.cos(phase)
    sine = jnp.sin(phase)
    turn_ref[0:half, :] = cosine
    turn_ref[half : 2 * half, :] = sine
    copies[4].wait()
    copies[5].wait()
    for j in range(8):
        packed[j * owned : (j + 1) * owned, :] = gains_ref[:, j, :]
        packed[(8 + j) * owned : (9 + j) * owned, :] = band_ref[:, j, :]
    for r in range(2):
        re = slice(r * half, (r + 1) * half)
        im = slice((2 + r) * half, (3 + r) * half)
        move_re = slice((4 + r) * half, (5 + r) * half)
        move_im = slice((6 + r) * half, (7 + r) * half)
        jones_re = cosine * packed[re, :] - sine * packed[im, :]
        jones_im = cosine * packed[im, :] + sine * packed[re, :]
        terms_ref[re, :] = jones_re
        terms_ref[im, :] = jones_im
        terms_ref[move_re, :] = (
            cosine * packed[move_re, :] - sine * packed[move_im, :] - rate * jones_im
        )
        terms_ref[move_im, :] = (
            cosine * packed[move_im, :] + sine * packed[move_re, :] + rate * jones_re
        )
    for copy in copies[6:]:
        copy.wait()


def times(a, b):
    out = []
    for r in range(2):
        for c in range(2):
            out.append(
                a[r * 2] * b[c] - a[4 + r * 2] * b[4 + c] + a[r * 2 + 1] * b[2 + c] - a[5 + r * 2] * b[6 + c]
            )
    for r in range(2):
        for c in range(2):
            out.append(
                a[r * 2] * b[4 + c] + a[4 + r * 2] * b[c] + a[r * 2 + 1] * b[6 + c] + a[5 + r * 2] * b[2 + c]
            )
    return out


def times_adjoint(a, b):
    out = []
    for r in range(2):
        for c in range(2):
            out.append(
                a[r * 2] * b[c * 2]
                + a[4 + r * 2] * b[4 + c * 2]
                + a[r * 2 + 1] * b[c * 2 + 1]
                + a[5 + r * 2] * b[5 + c * 2]
            )
    for r in range(2):
        for c in range(2):
            out.append(
                a[4 + r * 2] * b[c * 2]
                - a[r * 2] * b[4 + c * 2]
                + a[5 + r * 2] * b[c * 2 + 1]
                - a[r * 2 + 1] * b[5 + c * 2]
            )
    return out


def adjoint_times(a, b):
    out = []
    for r in range(2):
        for c in range(2):
            out.append(
                a[r] * b[c] + a[4 + r] * b[4 + c] + a[2 + r] * b[2 + c] + a[6 + r] * b[6 + c]
            )
    for r in range(2):
        for c in range(2):
            out.append(
                a[r] * b[4 + c] - a[4 + r] * b[c] + a[2 + r] * b[6 + c] - a[6 + r] * b[2 + c]
            )
    return out


def baseline_kernel(
    own_ref, even_ref, odd_ref, far_ref, model_ref, gather_ref, scatter_ref,
    even_out, group_out, table, picked, grads, model_parts, *, factor, blocks
):
    _, rows, width = model_parts.shape
    slots = table.shape[0]
    owned = slots // 4
    group = 32
    size = 8 * group
    place = group_place(blocks)
    odd_place = place + 1 - 2 * (place % 2)
    far_place = (place + 2) % 4
    partner = even_ref.at[1 - base_index() % 2]
    sources = (own_ref, partner, odd_ref, far_ref)
    for k, ref in enumerate(sources):
        for j in range(16):
            table[k * owned : (k + 1) * owned, j * width : (j + 1) * width] = ref[
                j * owned : (j + 1) * owned, :
            ]
    exact = table[...]
    high = exact.astype(bf16)
    rest = exact - high.astype(f32)
    middle = rest.astype(bf16)
    low = (rest - middle.astype(f32)).astype(bf16)
    split = jnp.concatenate(
        [high, middle, low, jnp.zeros((128 - 3 * slots, exact.shape[1]), bf16)], axis=0
    )
    out_row = lax.broadcasted_iota(jnp.int32, (size, size), 0)
    in_row = lax.broadcasted_iota(jnp.int32, (size, size), 1)
    wanted = (out_row % group) * 8 + out_row // group
    shuffle = jnp.where(in_row == wanted, 1.0, 0.0).astype(bf16)
    step = 2 * width
    cols = [slice(j * width, (j + 1) * width) for j in range(16)]
    stage = rows // 2
    def load(first):
        for g in range(first // group, (first + stage) // group):
            part = jnp.dot(
                shuffle, model_ref[g * size : (g + 1) * size, :], preferred_element_type=f32
            )
            for j in range(8):
                model_parts[j, g * group : (g + 1) * group, :] = part[j * group : (j + 1) * group, :]
        for base in (first, rows + first):
            pick = gather_ref[base : base + stage, :]
            for n in range(0, 16 * width, step):
                picked[base : base + stage, n : n + step] = jnp.dot(pick, split[:, n : n + step], preferred_element_type=f32)

    def chunk(i):
        at = slice(i * 8, i * 8 + 8)
        at_q = slice(rows + i * 8, rows + i * 8 + 8)
        model = [model_parts[j, at, :] for j in range(8)]
        right = times_adjoint(model, [picked[at_q, c] for c in cols[:8]])
        left = times([picked[at, c] for c in cols[:8]], model)
        one = times([picked[at, c] for c in cols[8:]], right)
        two = times_adjoint(left, [picked[at_q, c] for c in cols[8:]])
        change = [a + b for a, b in zip(one, two)]
        for c, value in zip(cols, times_adjoint(change, right)):
            grads[at, c] = value
        for c, value in zip(cols, adjoint_times(change, left)):
            grads[at_q, c] = value

    def collect(first):
        for n in range(0, 8 * width, step):
            total = None
            for base in (first, rows + first):
                value = grads[base : base + stage, n : n + step]
                sel = scatter_ref[:, base : base + stage]
                high = value.astype(bf16)
                low = (value - high.astype(f32)).astype(bf16)
                part = jnp.dot(sel, high, preferred_element_type=f32) + jnp.dot(
                    sel, low, preferred_element_type=f32
                )
                total = part if total is None else total + part
            if first:
                table[:, n : n + step] = table[:, n : n + step] + factor * total
            else:
                table[:, n : n + step] = factor * total

    load(0)
    for first in range(0, rows, stage):
        if first + stage < rows:
            load(first + stage)
        for i in range(first // 8, (first + stage) // 8):
            chunk(i)
        collect(first)
    group_out[(odd_place + 2) % 4] = jnp.zeros(even_out.shape, f32)
    sinks = (group_out.at[place], even_out, group_out.at[odd_place], group_out.at[far_place])
    for k, ref in enumerate(sinks):
        for j in range(8):
            ref[j * owned : (j + 1) * owned, :] = table[
                k * owned : (k + 1) * owned, j * width : (j + 1) * width
            ]


def curvature_kernel(
    even_ref, group_ref, terms_ref, turn_ref, small_ref, band_ref, res_ref,
    curv_ref, row_ref, *, channels
):
    owned, _, width = band_ref.shape
    half = 2 * owned
    delay_scale = channels ** (-0.5)
    freq = frequencies(chan_index(), width, channels)
    cosine = turn_ref[0:half, :]
    sine = turn_ref[half : 2 * half, :]
    total = even_ref[1 - base_index() % 2]
    for k in range(4):
        total = total + group_ref[k]
    moved = jnp.zeros((half, width), f32)
    for r in range(2):
        re = slice(r * half, (r + 1) * half)
        im = slice((2 + r) * half, (3 + r) * half)
        grad_re, grad_im = total[re, :], total[im, :]
        moved = moved + (terms_ref[re, :] * grad_im - terms_ref[im, :] * grad_re)
        band_re = cosine * grad_re + sine * grad_im
        band_im = cosine * grad_im - sine * grad_re
        for a in range(2):
            rows = slice(a * owned, (a + 1) * owned)
            j = 2 * r + a
            curv_ref[:, j, :] = band_re[rows, :] + damping_weight * band_ref[:, j, :]
            curv_ref[:, 4 + j, :] = band_im[rows, :] + damping_weight * band_ref[:, 4 + j, :]
    moved = jnp.sum(moved * (full_turn * delay_scale * freq), axis=1, keepdims=True)
    curv, band, res = curv_ref[...], band_ref[...], res_ref[...]
    scalars = [
        jnp.sum(jnp.sum(jnp.sum(x, axis=0), axis=0, keepdims=True), axis=1, keepdims=True)
        for x in (res * res, res * curv, curv * curv, band * curv)
    ]
    here = jnp.where(lax.axis_index("z") == 0, 1.0, 0.0)
    values = jnp.concatenate(
        [moved] + scalars + [jnp.zeros((4, 1), f32)]
        + [here * column(small_ref.at[0]), here * column(small_ref.at[1])],
        axis=0,
    )
    count = values.shape[0]
    diagonal = lax.broadcasted_iota(jnp.int32, (count, width), 0) == lax.broadcasted_iota(
        jnp.int32, (count, width), 1
    )
    row = jnp.sum(
        jnp.where(diagonal, jnp.broadcast_to(values, (count, width)), 0.0), axis=0, keepdims=True
    )
    row_ref[...] = jnp.broadcast_to(row, row_ref.shape)


def line_kernel(rows_ref, out_ref, *, across):
    count, width = rows_ref.shape
    lines, part = count // across, width // across
    lane = lax.broadcasted_iota(jnp.int32, (1, width), 1)
    total = jnp.zeros((1, width), f32)
    for x in range(across):
        line = jnp.sum(rows_ref[x * lines : (x + 1) * lines, :], axis=0, keepdims=True)
        line = jnp.where(lane < part, line, 0.0)
        total = total + (pltpu.roll(line, x * part, 1) if x else line)
    out_ref[...] = jnp.broadcast_to(total, out_ref.shape)


def update_kernel(
    rows_ref, curv_ref, small_ref, band_ref, res_ref, iter_ref,
    iter_out, iter_delay_out, res_out, res_delay_out, dir_out, dir_delay_out, *, across
):
    rows = rows_ref[...]
    count, width = rows.shape
    owned = band_ref.shape[0]
    half = 2 * owned
    sums = jnp.sum(rows, axis=0, keepdims=True)
    part = width // across
    lane = lax.broadcasted_iota(jnp.int32, (1, width), 1) % part

    def scalar(x):
        return jnp.sum(x, axis=1, keepdims=True)

    pair = rows + pltpu.roll(rows, count - 1, 0)
    moves = pltpu.roll(rows, width - 16, 1)
    lefts = pltpu.roll(rows, width - 24, 1)
    curves = pair + damping_weight * moves
    valid = (lax.broadcasted_iota(jnp.int32, (count, width), 0) % 2 == 0) & (
        lax.broadcasted_iota(jnp.int32, (count, width), 1) % part < half
    )

    def delays(x):
        return scalar(jnp.sum(jnp.where(valid, x, 0.0), axis=0, keepdims=True))

    squares = scalar(jnp.where(lane == half, sums, 0.0)) + delays(lefts * lefts)
    cross = scalar(jnp.where(lane == half + 1, sums, 0.0)) + delays(lefts * curves)
    norm = scalar(jnp.where(lane == half + 2, sums, 0.0)) + delays(curves * curves)
    curvature = scalar(jnp.where(lane == half + 3, sums, 0.0)) + delays(moves * curves)
    alpha = squares / curvature
    fresh = squares + alpha * (alpha * norm - 2.0 * cross)
    ratio = fresh / squares

    band, curv = band_ref[...], curv_ref[...]
    alpha3 = alpha.reshape(1, 1, 1)
    ratio3 = ratio.reshape(1, 1, 1)
    iter_out[...] = iter_ref[...] + alpha3 * band
    new_res = res_ref[...] - alpha3 * curv
    res_out[...] = new_res
    dir_out[...] = new_res + ratio3 * band

    mine = lax.broadcasted_iota(jnp.int32, (count, width), 0) == 2 * lax.axis_index("y")
    line = jnp.sum(jnp.where(mine, pair, 0.0), axis=0, keepdims=True)
    own = jnp.zeros((1, half), f32)
    for x in range(across):
        own = own + jnp.where(lax.axis_index("x") == x, line[:, x * part : x * part + half], 0.0)
    own = jnp.concatenate([own[:, 0:owned], own[:, owned:half]], axis=0)
    move = small_ref[0]
    iter_delay_out[...] = small_ref[2] + alpha * move
    new_left = small_ref[1] - alpha * (own + damping_weight * move)
    res_delay_out[...] = new_left
    dir_delay_out[...] = new_left + ratio * move


def body(
    gains,
    delays,
    model,
    antenna1,
    antenna2,
    dir_band,
    dir_delay,
    res_band,
    res_delay,
    iter_band,
    iter_delay,
):
    owned, _, width = gains.shape
    rows = model.shape[0]
    rings, lines = lax.axis_size("y"), lax.axis_size("z")
    across, cores = lax.axis_size("x"), lax.axis_size("core")
    blocks = rings * across
    base = ("y", "x")
    channels = width * lines * cores
    slots = 4 * owned
    factor = owned / (2.0 * rows)
    delays_t, dir_delay_t, res_delay_t, iter_delay_t = (
        jnp.transpose(x) for x in (delays, dir_delay, res_delay, iter_delay)
    )

    terms, turn, small, gather, scatter, model_local = pl.pallas_call(
        lambda *refs: station_kernel(*refs, channels=channels, blocks=blocks),
        out_shape=(
            shape(16 * owned, width),
            shape(4 * owned, width),
            shape(3, 2, owned),
            shape(2 * rows, 128, dtype=bf16),
            shape(slots, 2 * rows, dtype=bf16),
            shape(8 * rows, width, dtype=bf16),
        ),
        in_specs=[hbm()] * 9,
        out_specs=(vmem(),) * 6,
        scratch_shapes=[
            pltpu.VMEM((owned, 8, width), f32),
            pltpu.VMEM((owned, 8, width), f32),
            pltpu.VMEM((2, owned), f32),
            pltpu.VMEM((2, rows), jnp.int32),
            pltpu.VMEM((16 * owned, width), f32),
            pltpu.SemaphoreType.DMA((9,)),
        ],
        compiler_params=params(4),
        name="station_terms",
    )(
        *(
            pltpu.with_memory_space_constraint(x, pltpu.HBM)
            for x in (
                gains, dir_band, delays_t, dir_delay_t, res_delay_t, iter_delay_t,
                antenna1.reshape(1, rows), antenna2.reshape(1, rows), model.reshape(rows * 8, width),
            )
        )
    )

    even_groups = [[i, i + 1] for i in range(0, blocks, 2)]
    half = blocks // 2
    groups = [[i, i + 1, i + half, (i + 1 + half) % blocks] for i in range(1, half, 2)]

    def exchange(to_even, to_group):
        count = to_group.shape[1]
        group = lax.all_to_all(
            to_group.reshape(4 * count, width), base, 0, 0, axis_index_groups=groups, tiled=True
        )
        even = lax.all_gather(to_even, base, axis_index_groups=even_groups)
        return even, group.reshape(4, count, width)

    far_pairs = [(i, (i + half) % blocks) for i in range(blocks)]
    odd_pairs = [(i, (i + 1) % blocks if i % 2 else (i - 1) % blocks) for i in range(blocks)]
    from_far = lax.ppermute(terms, base, far_pairs)
    from_odd = lax.ppermute(terms, base, odd_pairs)
    from_even = lax.all_gather(terms, base, axis_index_groups=even_groups)

    to_even, to_group = pl.pallas_call(
        lambda *refs: baseline_kernel(*refs, factor=factor, blocks=blocks),
        out_shape=(shape(8 * owned, width), shape(4, 8 * owned, width)),
        in_specs=[vmem()] * 7,
        out_specs=(vmem(),) * 2,
        scratch_shapes=[
            pltpu.VMEM((slots, 16 * width), f32),
            pltpu.VMEM((2 * rows, 16 * width), f32),
            pltpu.VMEM((2 * rows, 8 * width), f32),
            pltpu.VMEM((8, rows, width), f32),
        ],
        compiler_params=params(24),
        name="baselines",
    )(terms, from_even, from_odd, from_far, model_local, gather, scatter)

    curv, row = pl.pallas_call(
        lambda *refs: curvature_kernel(*refs, channels=channels),
        out_shape=(shape(owned, 8, width), shape(across * lines, width)),
        in_specs=[vmem()] * 7,
        out_specs=(vmem(), vmem()),
        compiler_params=params(4),
        name="curvature",
    )(*exchange(to_even, to_group), terms, turn, small, dir_band, res_band)

    row = lax.all_to_all(row, ("x", "z"), 0, 0, tiled=True)
    row = pl.pallas_call(
        lambda *refs: line_kernel(*refs, across=across),
        out_shape=shape(rings * cores, width),
        in_specs=[vmem()],
        out_specs=vmem(),
        compiler_params=params(4),
        name="line_sums",
    )(row)
    everyone = lax.all_to_all(row, ("y", "core"), 0, 0, tiled=True)

    outs = pl.pallas_call(
        lambda *refs: update_kernel(*refs, across=across),
        out_shape=(
            shape(owned, 8, width),
            shape(2, owned),
            shape(owned, 8, width),
            shape(2, owned),
            shape(owned, 8, width),
            shape(2, owned),
        ),
        in_specs=[vmem()] * 6,
        out_specs=(vmem(),) * 6,
        compiler_params=params(4),
        name="update",
    )(everyone, curv, small, dir_band, res_band, iter_band)
    return (
        outs[0],
        jnp.transpose(outs[1]),
        outs[2],
        jnp.transpose(outs[3]),
        outs[4],
        jnp.transpose(outs[5]),
    )


def solution(mesh):
    cores, across = 2, 4
    blocks, chans = mesh.shape["base"], mesh.shape["chan"]
    split = Mesh(
        mesh.devices.reshape(blocks // across, across, chans // cores, cores), ("y", "x", "z", "core")
    )
    base, chan = ("y", "x"), ("z", "core")
    band = P(base, None, chan)
    delay = P(base, None)
    one = P(base)
    return jax.shard_map(
        body,
        mesh=split,
        in_specs=(band, delay, band, one, one, band, delay, band, delay, band, delay),
        out_specs=(band, delay) * 3,
        check_vma=False,
    )
```

```python
import math

import jax
import jax.numpy as jnp
from jax import lax
from jax.experimental import pallas as pl
from jax.experimental.pallas import tpu as pltpu
from jax.sharding import Mesh
from jax.sharding import PartitionSpec as P

full_turn = 2.0 * math.pi
damping_weight = 0.5

f32 = jnp.float32
bf16 = jnp.bfloat16


def vmem():
    return pl.BlockSpec(memory_space=pltpu.VMEM)


def hbm():
    return pl.BlockSpec(memory_space=pltpu.HBM)


def params(mib):
    return pltpu.CompilerParams(vmem_limit_bytes=int(mib * 1024 * 1024))


def shape(*dims, dtype=f32):
    return jax.ShapeDtypeStruct(dims, dtype)


def base_index():
    return lax.axis_index("y") * lax.axis_size("x") + lax.axis_index("x")


def group_place(blocks):
    block = base_index()
    first = jnp.where(block % 2 == 1, block, (block + blocks - 1) % blocks)
    return 1 - block % 2 + 2 * jnp.where(first >= blocks // 2, 1, 0)


def chan_index():
    return lax.axis_index("z") * lax.axis_size("core") + lax.axis_index("core")


def frequencies(chan, width, channels):
    index = lax.broadcasted_iota(jnp.int32, (1, width), 1) + chan * width
    return (index.astype(f32) + 0.5) / channels - 0.5


def column(row_ref):
    count = row_ref.shape[1]
    eye = lax.broadcasted_iota(jnp.int32, (count, count), 0) == lax.broadcasted_iota(
        jnp.int32, (count, count), 1
    )
    parts = [
        jnp.sum(
            jnp.where(eye, jnp.broadcast_to(row_ref[a : a + 1, :], (count, count)), 0.0),
            axis=1,
            keepdims=True,
        )
        for a in range(2)
    ]
    return jnp.concatenate(parts, axis=0)


def pick_stations(ids, gather_ref, scatter_ref, *, owned, blocks):
    rows = ids.shape[1]
    slots = 4 * owned
    slot = lax.broadcasted_iota(jnp.int32, (slots, 2 * rows), 0)
    kind = slot // owned
    block = base_index()
    turn_up = 1 - 2 * (block % 2)
    offset = jnp.where(kind == 0, 0, jnp.where(kind == 1, turn_up, jnp.where(kind == 2, -turn_up, blocks // 2)))
    station = ((block + offset + blocks) % blocks) * owned + slot % owned
    both = jnp.concatenate([ids[0:1, :], ids[1:2, :]], axis=1)
    pick = jnp.where(station == both, 1.0, 0.0)
    filled = jnp.concatenate([pick] * 3 + [jnp.zeros((128 - 3 * slots, 2 * rows), f32)], axis=0)
    scatter_ref[...] = pick.astype(bf16)
    gather_ref[...] = jnp.transpose(filled).astype(bf16)


def station_kernel(
    gains_hbm, band_hbm, delays_hbm, move_hbm, left_hbm, iter_hbm, first_hbm, second_hbm, model_hbm,
    terms_ref, turn_ref, small_ref, gather_ref, scatter_ref, model_ref,
    gains_ref, band_ref, delays_ref, ids, packed, sems, *, channels, blocks
):
    owned, _, width = gains_ref.shape
    rows = ids.shape[1]
    half = 2 * owned
    pairs = [
        (first_hbm, ids.at[0:1]),
        (second_hbm, ids.at[1:2]),
        (delays_hbm, delays_ref),
        (move_hbm, small_ref.at[0]),
        (gains_hbm, gains_ref),
        (band_hbm, band_ref),
    ]
    parts = 1
    share = 8 * rows // parts
    for k in range(parts):
        at = pl.ds(k * share, share)
        pairs.append((model_hbm.at[at], model_ref.at[at]))
    pairs += [(left_hbm, small_ref.at[1]), (iter_hbm, small_ref.at[2])]
    copies = [pltpu.make_async_copy(a, b, sems.at[k]) for k, (a, b) in enumerate(pairs)]
    for copy in copies:
        copy.start()
    copies[0].wait()
    copies[1].wait()
    pick_stations(ids, gather_ref, scatter_ref, owned=owned, blocks=blocks)
    copies[2].wait()
    copies[3].wait()
    delay_scale = channels ** (-0.5)
    freq = frequencies(chan_index(), width, channels)
    phase = full_turn * column(delays_ref) * freq
    rate = full_turn * delay_scale * column(small_ref.at[0]) * freq
    cosine = jnp.cos(phase)
    sine = jnp.sin(phase)
    turn_ref[0:half, :] = cosine
    turn_ref[half : 2 * half, :] = sine
    copies[4].wait()
    copies[5].wait()
    for j in range(8):
        packed[j * owned : (j + 1) * owned, :] = gains_ref[:, j, :]
        packed[(8 + j) * owned : (9 + j) * owned, :] = band_ref[:, j, :]
    for r in range(2):
        re = slice(r * half, (r + 1) * half)
        im = slice((2 + r) * half, (3 + r) * half)
        move_re = slice((4 + r) * half, (5 + r) * half)
        move_im = slice((6 + r) * half, (7 + r) * half)
        jones_re = cosine * packed[re, :] - sine * packed[im, :]
        jones_im = cosine * packed[im, :] + sine * packed[re, :]
        terms_ref[re, :] = jones_re
        terms_ref[im, :] = jones_im
        terms_ref[move_re, :] = (
            cosine * packed[move_re, :] - sine * packed[move_im, :] - rate * jones_im
        )
        terms_ref[move_im, :] = (
            cosine * packed[move_im, :] + sine * packed[move_re, :] + rate * jones_re
        )
    for copy in copies[6:]:
        copy.wait()


def times(a, b):
    out = []
    for r in range(2):
        for c in range(2):
            out.append(
                a[r * 2] * b[c] - a[4 + r * 2] * b[4 + c] + a[r * 2 + 1] * b[2 + c] - a[5 + r * 2] * b[6 + c]
            )
    for r in range(2):
        for c in range(2):
            out.append(
                a[r * 2] * b[4 + c] + a[4 + r * 2] * b[c] + a[r * 2 + 1] * b[6 + c] + a[5 + r * 2] * b[2 + c]
            )
    return out


def times_adjoint(a, b):
    out = []
    for r in range(2):
        for c in range(2):
            out.append(
                a[r * 2] * b[c * 2]
                + a[4 + r * 2] * b[4 + c * 2]
                + a[r * 2 + 1] * b[c * 2 + 1]
                + a[5 + r * 2] * b[5 + c * 2]
            )
    for r in range(2):
        for c in range(2):
            out.append(
                a[4 + r * 2] * b[c * 2]
                - a[r * 2] * b[4 + c * 2]
                + a[5 + r * 2] * b[c * 2 + 1]
                - a[r * 2 + 1] * b[5 + c * 2]
            )
    return out


def adjoint_times(a, b):
    out = []
    for r in range(2):
        for c in range(2):
            out.append(
                a[r] * b[c] + a[4 + r] * b[4 + c] + a[2 + r] * b[2 + c] + a[6 + r] * b[6 + c]
            )
    for r in range(2):
        for c in range(2):
            out.append(
                a[r] * b[4 + c] - a[4 + r] * b[c] + a[2 + r] * b[6 + c] - a[6 + r] * b[2 + c]
            )
    return out


def baseline_kernel(
    own_ref, even_ref, odd_ref, far_ref, model_ref, gather_ref, scatter_ref,
    even_out, group_hbm, table, picked, grads, model_parts, group_out, sems, *, factor, blocks
):
    _, rows, width = model_parts.shape
    slots = table.shape[0]
    owned = slots // 4
    group = 32
    size = 8 * group
    place = group_place(blocks)
    odd_place = place + 1 - 2 * (place % 2)
    far_place = (place + 2) % 4
    partner = even_ref.at[1 - base_index() % 2]
    sources = (own_ref, partner, odd_ref, far_ref)
    for k, ref in enumerate(sources):
        for j in range(16):
            table[k * owned : (k + 1) * owned, j * width : (j + 1) * width] = ref[
                j * owned : (j + 1) * owned, :
            ]
    exact = table[...]
    high = exact.astype(bf16)
    rest = exact - high.astype(f32)
    middle = rest.astype(bf16)
    low = (rest - middle.astype(f32)).astype(bf16)
    split = jnp.concatenate(
        [high, middle, low, jnp.zeros((128 - 3 * slots, exact.shape[1]), bf16)], axis=0
    )
    out_row = lax.broadcasted_iota(jnp.int32, (size, size), 0)
    in_row = lax.broadcasted_iota(jnp.int32, (size, size), 1)
    wanted = (out_row % group) * 8 + out_row // group
    shuffle = jnp.where(in_row == wanted, 1.0, 0.0).astype(bf16)
    step = 2 * width
    cols = [slice(j * width, (j + 1) * width) for j in range(16)]
    stage = rows // 2
    def load(first):
        for g in range(first // group, (first + stage) // group):
            part = jnp.dot(
                shuffle, model_ref[g * size : (g + 1) * size, :], preferred_element_type=f32
            )
            for j in range(8):
                model_parts[j, g * group : (g + 1) * group, :] = part[j * group : (j + 1) * group, :]
        for base in (first, rows + first):
            pick = gather_ref[base : base + stage, :]
            for n in range(0, 16 * width, step):
                picked[base : base + stage, n : n + step] = jnp.dot(pick, split[:, n : n + step], preferred_element_type=f32)

    def chunk(i):
        at = slice(i * 8, i * 8 + 8)
        at_q = slice(rows + i * 8, rows + i * 8 + 8)
        model = [model_parts[j, at, :] for j in range(8)]
        right = times_adjoint(model, [picked[at_q, c] for c in cols[:8]])
        left = times([picked[at, c] for c in cols[:8]], model)
        one = times([picked[at, c] for c in cols[8:]], right)
        two = times_adjoint(left, [picked[at_q, c] for c in cols[8:]])
        change = [a + b for a, b in zip(one, two)]
        for c, value in zip(cols, times_adjoint(change, right)):
            grads[at, c] = value
        for c, value in zip(cols, adjoint_times(change, left)):
            grads[at_q, c] = value

    def collect(first, then):
        for n in range(0, 8 * width, step):
            total = None
            for base in (first, rows + first):
                value = grads[base : base + stage, n : n + step]
                sel = scatter_ref[:, base : base + stage]
                high = value.astype(bf16)
                low = (value - high.astype(f32)).astype(bf16)
                part = jnp.dot(sel, high, preferred_element_type=f32) + jnp.dot(
                    sel, low, preferred_element_type=f32
                )
                total = part if total is None else total + part
            if first:
                table[:, n : n + step] = table[:, n : n + step] + factor * total
            else:
                table[:, n : n + step] = factor * total
            if then is not None:
                then(n)

    group_out[(odd_place + 2) % 4] = jnp.zeros(even_out.shape, f32)
    sinks = (group_out.at[place], even_out, group_out.at[odd_place], group_out.at[far_place])
    copies = []

    def deliver(n):
        first = n // width
        for k, ref in enumerate(sinks):
            for j in (first, first + 1):
                ref[j * owned : (j + 1) * owned, :] = table[
                    k * owned : (k + 1) * owned, j * width : (j + 1) * width
                ]
        at = pl.ds(first * owned, 2 * owned)
        copy = pltpu.make_async_copy(
            group_out.at[:, at, :], group_hbm.at[:, at, :], sems.at[n // step]
        )
        copy.start()
        copies.append(copy)

    load(0)
    for first in range(0, rows, stage):
        if first + stage < rows:
            load(first + stage)
        for i in range(first // 8, (first + stage) // 8):
            chunk(i)
        last = first + stage == rows
        collect(first, deliver if last else None)
    for copy in copies:
        copy.wait()


def curvature_kernel(
    even_ref, group_ref, terms_ref, turn_ref, small_ref, band_ref, res_ref,
    curv_ref, row_ref, *, channels
):
    owned, _, width = band_ref.shape
    half = 2 * owned
    delay_scale = channels ** (-0.5)
    freq = frequencies(chan_index(), width, channels)
    cosine = turn_ref[0:half, :]
    sine = turn_ref[half : 2 * half, :]
    total = even_ref[1 - base_index() % 2]
    for k in range(4):
        total = total + group_ref[k]
    moved = jnp.zeros((half, width), f32)
    for r in range(2):
        re = slice(r * half, (r + 1) * half)
        im = slice((2 + r) * half, (3 + r) * half)
        grad_re, grad_im = total[re, :], total[im, :]
        moved = moved + (terms_ref[re, :] * grad_im - terms_ref[im, :] * grad_re)
        band_re = cosine * grad_re + sine * grad_im
        band_im = cosine * grad_im - sine * grad_re
        for a in range(2):
            rows = slice(a * owned, (a + 1) * owned)
            j = 2 * r + a
            curv_ref[:, j, :] = band_re[rows, :] + damping_weight * band_ref[:, j, :]
            curv_ref[:, 4 + j, :] = band_im[rows, :] + damping_weight * band_ref[:, 4 + j, :]
    moved = jnp.sum(moved * (full_turn * delay_scale * freq), axis=1, keepdims=True)
    curv, band, res = curv_ref[...], band_ref[...], res_ref[...]
    scalars = [
        jnp.sum(jnp.sum(jnp.sum(x, axis=0), axis=0, keepdims=True), axis=1, keepdims=True)
        for x in (res * res, res * curv, curv * curv, band * curv)
    ]
    here = jnp.where(lax.axis_index("z") == 0, 1.0, 0.0)
    values = jnp.concatenate(
        [moved] + scalars + [jnp.zeros((4, 1), f32)]
        + [here * column(small_ref.at[0]), here * column(small_ref.at[1])],
        axis=0,
    )
    count = values.shape[0]
    diagonal = lax.broadcasted_iota(jnp.int32, (count, width), 0) == lax.broadcasted_iota(
        jnp.int32, (count, width), 1
    )
    row = jnp.sum(
        jnp.where(diagonal, jnp.broadcast_to(values, (count, width)), 0.0), axis=0, keepdims=True
    )
    row_ref[...] = jnp.broadcast_to(row, row_ref.shape)


def line_kernel(rows_ref, out_ref, *, across):
    count, width = rows_ref.shape
    lines, part = count // across, width // across
    lane = lax.broadcasted_iota(jnp.int32, (1, width), 1)
    total = jnp.zeros((1, width), f32)
    for x in range(across):
        line = jnp.sum(rows_ref[x * lines : (x + 1) * lines, :], axis=0, keepdims=True)
        line = jnp.where(lane < part, line, 0.0)
        total = total + (pltpu.roll(line, x * part, 1) if x else line)
    out_ref[...] = jnp.broadcast_to(total, out_ref.shape)


def update_kernel(
    rows_ref, curv_ref, small_ref, band_ref, res_ref, iter_ref,
    iter_out, iter_delay_out, res_out, res_delay_out, dir_out, dir_delay_out, *, across
):
    rows = rows_ref[...]
    count, width = rows.shape
    owned = band_ref.shape[0]
    half = 2 * owned
    sums = jnp.sum(rows, axis=0, keepdims=True)
    part = width // across
    lane = lax.broadcasted_iota(jnp.int32, (1, width), 1) % part

    def scalar(x):
        return jnp.sum(x, axis=1, keepdims=True)

    pair = rows + pltpu.roll(rows, count - 1, 0)
    moves = pltpu.roll(rows, width - 16, 1)
    lefts = pltpu.roll(rows, width - 24, 1)
    curves = pair + damping_weight * moves
    valid = (lax.broadcasted_iota(jnp.int32, (count, width), 0) % 2 == 0) & (
        lax.broadcasted_iota(jnp.int32, (count, width), 1) % part < half
    )

    def delays(x):
        return scalar(jnp.sum(jnp.where(valid, x, 0.0), axis=0, keepdims=True))

    squares = scalar(jnp.where(lane == half, sums, 0.0)) + delays(lefts * lefts)
    cross = scalar(jnp.where(lane == half + 1, sums, 0.0)) + delays(lefts * curves)
    norm = scalar(jnp.where(lane == half + 2, sums, 0.0)) + delays(curves * curves)
    curvature = scalar(jnp.where(lane == half + 3, sums, 0.0)) + delays(moves * curves)
    alpha = squares / curvature
    fresh = squares + alpha * (alpha * norm - 2.0 * cross)
    ratio = fresh / squares

    band, curv = band_ref[...], curv_ref[...]
    alpha3 = alpha.reshape(1, 1, 1)
    ratio3 = ratio.reshape(1, 1, 1)
    iter_out[...] = iter_ref[...] + alpha3 * band
    new_res = res_ref[...] - alpha3 * curv
    res_out[...] = new_res
    dir_out[...] = new_res + ratio3 * band

    mine = lax.broadcasted_iota(jnp.int32, (count, width), 0) == 2 * lax.axis_index("y")
    line = jnp.sum(jnp.where(mine, pair, 0.0), axis=0, keepdims=True)
    own = jnp.zeros((1, half), f32)
    for x in range(across):
        own = own + jnp.where(lax.axis_index("x") == x, line[:, x * part : x * part + half], 0.0)
    own = jnp.concatenate([own[:, 0:owned], own[:, owned:half]], axis=0)
    move = small_ref[0]
    iter_delay_out[...] = small_ref[2] + alpha * move
    new_left = small_ref[1] - alpha * (own + damping_weight * move)
    res_delay_out[...] = new_left
    dir_delay_out[...] = new_left + ratio * move


def body(
    gains,
    delays,
    model,
    antenna1,
    antenna2,
    dir_band,
    dir_delay,
    res_band,
    res_delay,
    iter_band,
    iter_delay,
):
    owned, _, width = gains.shape
    rows = model.shape[0]
    rings, lines = lax.axis_size("y"), lax.axis_size("z")
    across, cores = lax.axis_size("x"), lax.axis_size("core")
    blocks = rings * across
    base = ("y", "x")
    channels = width * lines * cores
    slots = 4 * owned
    factor = owned / (2.0 * rows)
    delays_t, dir_delay_t, res_delay_t, iter_delay_t = (
        jnp.transpose(x) for x in (delays, dir_delay, res_delay, iter_delay)
    )

    terms, turn, small, gather, scatter, model_local = pl.pallas_call(
        lambda *refs: station_kernel(*refs, channels=channels, blocks=blocks),
        out_shape=(
            shape(16 * owned, width),
            shape(4 * owned, width),
            shape(3, 2, owned),
            shape(2 * rows, 128, dtype=bf16),
            shape(slots, 2 * rows, dtype=bf16),
            shape(8 * rows, width, dtype=bf16),
        ),
        in_specs=[hbm()] * 9,
        out_specs=(vmem(),) * 6,
        scratch_shapes=[
            pltpu.VMEM((owned, 8, width), f32),
            pltpu.VMEM((owned, 8, width), f32),
            pltpu.VMEM((2, owned), f32),
            pltpu.VMEM((2, rows), jnp.int32),
            pltpu.VMEM((16 * owned, width), f32),
            pltpu.SemaphoreType.DMA((9,)),
        ],
        compiler_params=params(4),
        name="station_terms",
    )(
        *(
            pltpu.with_memory_space_constraint(x, pltpu.HBM)
            for x in (
                gains, dir_band, delays_t, dir_delay_t, res_delay_t, iter_delay_t,
                antenna1.reshape(1, rows), antenna2.reshape(1, rows), model.reshape(rows * 8, width),
            )
        )
    )

    even_groups = [[i, i + 1] for i in range(0, blocks, 2)]
    half = blocks // 2
    groups = [[i, i + 1, i + half, (i + 1 + half) % blocks] for i in range(1, half, 2)]

    def exchange(to_even, to_group):
        count = to_group.shape[1]
        group = lax.all_to_all(
            to_group.reshape(4 * count, width), base, 0, 0, axis_index_groups=groups, tiled=True
        )
        even = lax.all_gather(to_even, base, axis_index_groups=even_groups)
        return even, group.reshape(4, count, width)

    far_pairs = [(i, (i + half) % blocks) for i in range(blocks)]
    odd_pairs = [(i, (i + 1) % blocks if i % 2 else (i - 1) % blocks) for i in range(blocks)]
    from_far = lax.ppermute(terms, base, far_pairs)
    from_odd = lax.ppermute(terms, base, odd_pairs)
    from_even = lax.all_gather(terms, base, axis_index_groups=even_groups)

    to_even, to_group = pl.pallas_call(
        lambda *refs: baseline_kernel(*refs, factor=factor, blocks=blocks),
        out_shape=(shape(8 * owned, width), shape(4, 8 * owned, width)),
        in_specs=[vmem()] * 7,
        out_specs=(vmem(), hbm()),
        scratch_shapes=[
            pltpu.VMEM((slots, 16 * width), f32),
            pltpu.VMEM((2 * rows, 16 * width), f32),
            pltpu.VMEM((2 * rows, 8 * width), f32),
            pltpu.VMEM((8, rows, width), f32),
            pltpu.VMEM((4, 8 * owned, width), f32),
            pltpu.SemaphoreType.DMA((4,)),
        ],
        compiler_params=params(24),
        name="baselines",
    )(terms, from_even, from_odd, from_far, model_local, gather, scatter)

    curv, row = pl.pallas_call(
        lambda *refs: curvature_kernel(*refs, channels=channels),
        out_shape=(shape(owned, 8, width), shape(across * lines, width)),
        in_specs=[vmem()] * 7,
        out_specs=(vmem(), vmem()),
        compiler_params=params(4),
        name="curvature",
    )(*exchange(to_even, to_group), terms, turn, small, dir_band, res_band)

    row = lax.all_to_all(row, ("x", "z"), 0, 0, tiled=True)
    row = pl.pallas_call(
        lambda *refs: line_kernel(*refs, across=across),
        out_shape=shape(rings * cores, width),
        in_specs=[vmem()],
        out_specs=vmem(),
        compiler_params=params(4),
        name="line_sums",
    )(row)
    everyone = lax.all_to_all(row, ("y", "core"), 0, 0, tiled=True)

    outs = pl.pallas_call(
        lambda *refs: update_kernel(*refs, across=across),
        out_shape=(
            shape(owned, 8, width),
            shape(2, owned),
            shape(owned, 8, width),
            shape(2, owned),
            shape(owned, 8, width),
            shape(2, owned),
        ),
        in_specs=[vmem()] * 6,
        out_specs=(vmem(),) * 6,
        compiler_params=params(4),
        name="update",
    )(everyone, curv, small, dir_band, res_band, iter_band)
    return (
        outs[0],
        jnp.transpose(outs[1]),
        outs[2],
        jnp.transpose(outs[3]),
        outs[4],
        jnp.transpose(outs[5]),
    )


def solution(mesh):
    cores, across = 2, 4
    blocks, chans = mesh.shape["base"], mesh.shape["chan"]
    split = Mesh(
        mesh.devices.reshape(blocks // across, across, chans // cores, cores), ("y", "x", "z", "core")
    )
    base, chan = ("y", "x"), ("z", "core")
    band = P(base, None, chan)
    delay = P(base, None)
    one = P(base)
    return jax.shard_map(
        body,
        mesh=split,
        in_specs=(band, delay, band, one, one, band, delay, band, delay, band, delay),
        out_specs=(band, delay) * 3,
        check_vma=False,
    )
```

```python
import math

import jax
import jax.numpy as jnp
from jax import lax
from jax.experimental import pallas as pl
from jax.experimental.pallas import tpu as pltpu
from jax.sharding import Mesh
from jax.sharding import PartitionSpec as P

full_turn = 2.0 * math.pi
damping_weight = 0.5

f32 = jnp.float32
bf16 = jnp.bfloat16


def vmem():
    return pl.BlockSpec(memory_space=pltpu.VMEM)


def hbm():
    return pl.BlockSpec(memory_space=pltpu.HBM)


def params(mib):
    return pltpu.CompilerParams(vmem_limit_bytes=int(mib * 1024 * 1024))


def shape(*dims, dtype=f32):
    return jax.ShapeDtypeStruct(dims, dtype)


def base_index():
    return lax.axis_index("y") * lax.axis_size("x") + lax.axis_index("x")


def group_place(blocks):
    block = base_index()
    first = jnp.where(block % 2 == 1, block, (block + blocks - 1) % blocks)
    return 1 - block % 2 + 2 * jnp.where(first >= blocks // 2, 1, 0)


def chan_index():
    return lax.axis_index("z") * lax.axis_size("core") + lax.axis_index("core")


def frequencies(chan, width, channels):
    index = lax.broadcasted_iota(jnp.int32, (1, width), 1) + chan * width
    return (index.astype(f32) + 0.5) / channels - 0.5


def column(row_ref):
    count = row_ref.shape[1]
    eye = lax.broadcasted_iota(jnp.int32, (count, count), 0) == lax.broadcasted_iota(
        jnp.int32, (count, count), 1
    )
    parts = [
        jnp.sum(
            jnp.where(eye, jnp.broadcast_to(row_ref[a : a + 1, :], (count, count)), 0.0),
            axis=1,
            keepdims=True,
        )
        for a in range(2)
    ]
    return jnp.concatenate(parts, axis=0)


def pick_stations(ids, gather_ref, scatter_ref, *, owned, blocks):
    rows = ids.shape[1]
    slots = 4 * owned
    slot = lax.broadcasted_iota(jnp.int32, (slots, 2 * rows), 0)
    kind = slot // owned
    block = base_index()
    turn_up = 1 - 2 * (block % 2)
    offset = jnp.where(kind == 0, 0, jnp.where(kind == 1, turn_up, jnp.where(kind == 2, -turn_up, blocks // 2)))
    station = ((block + offset + blocks) % blocks) * owned + slot % owned
    both = jnp.concatenate([ids[0:1, :], ids[1:2, :]], axis=1)
    pick = jnp.where(station == both, 1.0, 0.0)
    filled = jnp.concatenate([pick] * 3 + [jnp.zeros((128 - 3 * slots, 2 * rows), f32)], axis=0)
    scatter_ref[...] = pick.astype(bf16)
    gather_ref[...] = jnp.transpose(filled).astype(bf16)


def station_kernel(
    gains_hbm, band_hbm, delays_hbm, move_hbm, left_hbm, iter_hbm, first_hbm, second_hbm, model_hbm,
    terms_ref, turn_ref, small_ref, gather_ref, scatter_ref, model_ref,
    gains_ref, band_ref, delays_ref, ids, packed, sems, *, channels, blocks
):
    owned, _, width = gains_ref.shape
    rows = ids.shape[1]
    half = 2 * owned
    pairs = [
        (first_hbm, ids.at[0:1]),
        (second_hbm, ids.at[1:2]),
        (delays_hbm, delays_ref),
        (move_hbm, small_ref.at[0]),
        (gains_hbm, gains_ref),
        (band_hbm, band_ref),
    ]
    parts = 1
    share = 8 * rows // parts
    for k in range(parts):
        at = pl.ds(k * share, share)
        pairs.append((model_hbm.at[at], model_ref.at[at]))
    pairs += [(left_hbm, small_ref.at[1]), (iter_hbm, small_ref.at[2])]
    copies = [pltpu.make_async_copy(a, b, sems.at[k]) for k, (a, b) in enumerate(pairs)]
    for copy in copies:
        copy.start()
    copies[0].wait()
    copies[1].wait()
    pick_stations(ids, gather_ref, scatter_ref, owned=owned, blocks=blocks)
    copies[2].wait()
    copies[3].wait()
    delay_scale = channels ** (-0.5)
    freq = frequencies(chan_index(), width, channels)
    phase = full_turn * column(delays_ref) * freq
    rate = full_turn * delay_scale * column(small_ref.at[0]) * freq
    cosine = jnp.cos(phase)
    sine = jnp.sin(phase)
    turn_ref[0:half, :] = cosine
    turn_ref[half : 2 * half, :] = sine
    copies[4].wait()
    copies[5].wait()
    for j in range(8):
        packed[j * owned : (j + 1) * owned, :] = gains_ref[:, j, :]
        packed[(8 + j) * owned : (9 + j) * owned, :] = band_ref[:, j, :]
    for r in range(2):
        re = slice(r * half, (r + 1) * half)
        im = slice((2 + r) * half, (3 + r) * half)
        move_re = slice((4 + r) * half, (5 + r) * half)
        move_im = slice((6 + r) * half, (7 + r) * half)
        jones_re = cosine * packed[re, :] - sine * packed[im, :]
        jones_im = cosine * packed[im, :] + sine * packed[re, :]
        terms_ref[re, :] = jones_re
        terms_ref[im, :] = jones_im
        terms_ref[move_re, :] = (
            cosine * packed[move_re, :] - sine * packed[move_im, :] - rate * jones_im
        )
        terms_ref[move_im, :] = (
            cosine * packed[move_im, :] + sine * packed[move_re, :] + rate * jones_re
        )
    for copy in copies[6:]:
        copy.wait()


def times(a, b):
    out = []
    for r in range(2):
        for c in range(2):
            out.append(
                a[r * 2] * b[c] - a[4 + r * 2] * b[4 + c] + a[r * 2 + 1] * b[2 + c] - a[5 + r * 2] * b[6 + c]
            )
    for r in range(2):
        for c in range(2):
            out.append(
                a[r * 2] * b[4 + c] + a[4 + r * 2] * b[c] + a[r * 2 + 1] * b[6 + c] + a[5 + r * 2] * b[2 + c]
            )
    return out


def times_adjoint(a, b):
    out = []
    for r in range(2):
        for c in range(2):
            out.append(
                a[r * 2] * b[c * 2]
                + a[4 + r * 2] * b[4 + c * 2]
                + a[r * 2 + 1] * b[c * 2 + 1]
                + a[5 + r * 2] * b[5 + c * 2]
            )
    for r in range(2):
        for c in range(2):
            out.append(
                a[4 + r * 2] * b[c * 2]
                - a[r * 2] * b[4 + c * 2]
                + a[5 + r * 2] * b[c * 2 + 1]
                - a[r * 2 + 1] * b[5 + c * 2]
            )
    return out


def adjoint_times(a, b):
    out = []
    for r in range(2):
        for c in range(2):
            out.append(
                a[r] * b[c] + a[4 + r] * b[4 + c] + a[2 + r] * b[2 + c] + a[6 + r] * b[6 + c]
            )
    for r in range(2):
        for c in range(2):
            out.append(
                a[r] * b[4 + c] - a[4 + r] * b[c] + a[2 + r] * b[6 + c] - a[6 + r] * b[2 + c]
            )
    return out


def baseline_kernel(
    own_ref, even_ref, odd_ref, far_ref, model_ref, gather_ref, scatter_ref,
    even_out, group_out, table, picked, grads, model_parts, *, factor, blocks
):
    _, rows, width = model_parts.shape
    slots = table.shape[0]
    owned = slots // 4
    group = 32
    size = 8 * group
    place = group_place(blocks)
    odd_place = place + 1 - 2 * (place % 2)
    far_place = (place + 2) % 4
    partner = even_ref.at[1 - base_index() % 2]
    sources = (own_ref, partner, odd_ref, far_ref)
    for k, ref in enumerate(sources):
        for j in range(16):
            table[k * owned : (k + 1) * owned, j * width : (j + 1) * width] = ref[
                j * owned : (j + 1) * owned, :
            ]
    exact = table[...]
    high = exact.astype(bf16)
    rest = exact - high.astype(f32)
    middle = rest.astype(bf16)
    low = (rest - middle.astype(f32)).astype(bf16)
    split = jnp.concatenate(
        [high, middle, low, jnp.zeros((128 - 3 * slots, exact.shape[1]), bf16)], axis=0
    )
    out_row = lax.broadcasted_iota(jnp.int32, (size, size), 0)
    in_row = lax.broadcasted_iota(jnp.int32, (size, size), 1)
    wanted = (out_row % group) * 8 + out_row // group
    shuffle = jnp.where(in_row == wanted, 1.0, 0.0).astype(bf16)
    step = 2 * width
    cols = [slice(j * width, (j + 1) * width) for j in range(16)]
    stage = rows // 2
    def load(first):
        for g in range(first // group, (first + stage) // group, 2):
            both = jnp.concatenate(
                [model_ref[k * size : (k + 1) * size, :] for k in (g, g + 1)], axis=1
            )
            part = jnp.dot(shuffle, both, preferred_element_type=f32)
            for j in range(8):
                for k in range(2):
                    model_parts[j, (g + k) * group : (g + k + 1) * group, :] = part[
                        j * group : (j + 1) * group, k * width : (k + 1) * width
                    ]
        for base in (first, rows + first):
            pick = gather_ref[base : base + stage, :]
            for n in range(0, 16 * width, step):
                picked[base : base + stage, n : n + step] = jnp.dot(pick, split[:, n : n + step], preferred_element_type=f32)

    def chunk(i):
        at = slice(i * 8, i * 8 + 8)
        at_q = slice(rows + i * 8, rows + i * 8 + 8)
        model = [model_parts[j, at, :] for j in range(8)]
        right = times_adjoint(model, [picked[at_q, c] for c in cols[:8]])
        left = times([picked[at, c] for c in cols[:8]], model)
        one = times([picked[at, c] for c in cols[8:]], right)
        two = times_adjoint(left, [picked[at_q, c] for c in cols[8:]])
        change = [a + b for a, b in zip(one, two)]
        for c, value in zip(cols, times_adjoint(change, right)):
            grads[at, c] = value
        for c, value in zip(cols, adjoint_times(change, left)):
            grads[at_q, c] = value

    def collect(first):
        for n in range(0, 8 * width, step):
            total = None
            for base in (first, rows + first):
                value = grads[base : base + stage, n : n + step]
                sel = scatter_ref[:, base : base + stage]
                high = value.astype(bf16)
                low = (value - high.astype(f32)).astype(bf16)
                part = jnp.dot(
                    jnp.concatenate([sel, sel], axis=1),
                    jnp.concatenate([high, low], axis=0),
                    preferred_element_type=f32,
                )
                total = part if total is None else total + part
            if first:
                table[:, n : n + step] = table[:, n : n + step] + factor * total
            else:
                table[:, n : n + step] = factor * total

    load(0)
    for first in range(0, rows, stage):
        if first + stage < rows:
            load(first + stage)
        for i in range(first // 8, (first + stage) // 8):
            chunk(i)
        collect(first)
    group_out[(odd_place + 2) % 4] = jnp.zeros(even_out.shape, f32)
    sinks = (group_out.at[place], even_out, group_out.at[odd_place], group_out.at[far_place])
    for k, ref in enumerate(sinks):
        for j in range(8):
            ref[j * owned : (j + 1) * owned, :] = table[
                k * owned : (k + 1) * owned, j * width : (j + 1) * width
            ]


def curvature_kernel(
    even_ref, group_ref, terms_ref, turn_ref, small_ref, band_ref, res_ref,
    curv_ref, row_ref, *, channels
):
    owned, _, width = band_ref.shape
    half = 2 * owned
    delay_scale = channels ** (-0.5)
    freq = frequencies(chan_index(), width, channels)
    cosine = turn_ref[0:half, :]
    sine = turn_ref[half : 2 * half, :]
    total = even_ref[1 - base_index() % 2]
    for k in range(4):
        total = total + group_ref[k]
    moved = jnp.zeros((half, width), f32)
    for r in range(2):
        re = slice(r * half, (r + 1) * half)
        im = slice((2 + r) * half, (3 + r) * half)
        grad_re, grad_im = total[re, :], total[im, :]
        moved = moved + (terms_ref[re, :] * grad_im - terms_ref[im, :] * grad_re)
        band_re = cosine * grad_re + sine * grad_im
        band_im = cosine * grad_im - sine * grad_re
        for a in range(2):
            rows = slice(a * owned, (a + 1) * owned)
            j = 2 * r + a
            curv_ref[:, j, :] = band_re[rows, :] + damping_weight * band_ref[:, j, :]
            curv_ref[:, 4 + j, :] = band_im[rows, :] + damping_weight * band_ref[:, 4 + j, :]
    moved = jnp.sum(moved * (full_turn * delay_scale * freq), axis=1, keepdims=True)
    curv, band, res = curv_ref[...], band_ref[...], res_ref[...]
    scalars = [
        jnp.sum(jnp.sum(jnp.sum(x, axis=0), axis=0, keepdims=True), axis=1, keepdims=True)
        for x in (res * res, res * curv, curv * curv, band * curv)
    ]
    here = jnp.where(lax.axis_index("z") == 0, 1.0, 0.0)
    values = jnp.concatenate(
        [moved] + scalars + [jnp.zeros((4, 1), f32)]
        + [here * column(small_ref.at[0]), here * column(small_ref.at[1])],
        axis=0,
    )
    count = values.shape[0]
    diagonal = lax.broadcasted_iota(jnp.int32, (count, width), 0) == lax.broadcasted_iota(
        jnp.int32, (count, width), 1
    )
    row = jnp.sum(
        jnp.where(diagonal, jnp.broadcast_to(values, (count, width)), 0.0), axis=0, keepdims=True
    )
    row_ref[...] = jnp.broadcast_to(row, row_ref.shape)


def line_kernel(rows_ref, out_ref, *, across):
    count, width = rows_ref.shape
    lines, part = count // across, width // across
    lane = lax.broadcasted_iota(jnp.int32, (1, width), 1)
    total = jnp.zeros((1, width), f32)
    for x in range(across):
        line = jnp.sum(rows_ref[x * lines : (x + 1) * lines, :], axis=0, keepdims=True)
        line = jnp.where(lane < part, line, 0.0)
        total = total + (pltpu.roll(line, x * part, 1) if x else line)
    out_ref[...] = jnp.broadcast_to(total, out_ref.shape)


def update_kernel(
    rows_ref, curv_ref, small_ref, band_ref, res_ref, iter_ref,
    iter_out, iter_delay_out, res_out, res_delay_out, dir_out, dir_delay_out, *, across
):
    rows = rows_ref[...]
    count, width = rows.shape
    owned = band_ref.shape[0]
    half = 2 * owned
    sums = jnp.sum(rows, axis=0, keepdims=True)
    part = width // across
    lane = lax.broadcasted_iota(jnp.int32, (1, width), 1) % part

    def scalar(x):
        return jnp.sum(x, axis=1, keepdims=True)

    pair = rows + pltpu.roll(rows, count - 1, 0)
    moves = pltpu.roll(rows, width - 16, 1)
    lefts = pltpu.roll(rows, width - 24, 1)
    curves = pair + damping_weight * moves
    valid = (lax.broadcasted_iota(jnp.int32, (count, width), 0) % 2 == 0) & (
        lax.broadcasted_iota(jnp.int32, (count, width), 1) % part < half
    )

    def delays(x):
        return scalar(jnp.sum(jnp.where(valid, x, 0.0), axis=0, keepdims=True))

    squares = scalar(jnp.where(lane == half, sums, 0.0)) + delays(lefts * lefts)
    cross = scalar(jnp.where(lane == half + 1, sums, 0.0)) + delays(lefts * curves)
    norm = scalar(jnp.where(lane == half + 2, sums, 0.0)) + delays(curves * curves)
    curvature = scalar(jnp.where(lane == half + 3, sums, 0.0)) + delays(moves * curves)
    alpha = squares / curvature
    fresh = squares + alpha * (alpha * norm - 2.0 * cross)
    ratio = fresh / squares

    band, curv = band_ref[...], curv_ref[...]
    alpha3 = alpha.reshape(1, 1, 1)
    ratio3 = ratio.reshape(1, 1, 1)
    iter_out[...] = iter_ref[...] + alpha3 * band
    new_res = res_ref[...] - alpha3 * curv
    res_out[...] = new_res
    dir_out[...] = new_res + ratio3 * band

    mine = lax.broadcasted_iota(jnp.int32, (count, width), 0) == 2 * lax.axis_index("y")
    line = jnp.sum(jnp.where(mine, pair, 0.0), axis=0, keepdims=True)
    own = jnp.zeros((1, half), f32)
    for x in range(across):
        own = own + jnp.where(lax.axis_index("x") == x, line[:, x * part : x * part + half], 0.0)
    own = jnp.concatenate([own[:, 0:owned], own[:, owned:half]], axis=0)
    move = small_ref[0]
    iter_delay_out[...] = small_ref[2] + alpha * move
    new_left = small_ref[1] - alpha * (own + damping_weight * move)
    res_delay_out[...] = new_left
    dir_delay_out[...] = new_left + ratio * move


def body(
    gains,
    delays,
    model,
    antenna1,
    antenna2,
    dir_band,
    dir_delay,
    res_band,
    res_delay,
    iter_band,
    iter_delay,
):
    owned, _, width = gains.shape
    rows = model.shape[0]
    rings, lines = lax.axis_size("y"), lax.axis_size("z")
    across, cores = lax.axis_size("x"), lax.axis_size("core")
    blocks = rings * across
    base = ("y", "x")
    channels = width * lines * cores
    slots = 4 * owned
    factor = owned / (2.0 * rows)
    delays_t, dir_delay_t, res_delay_t, iter_delay_t = (
        jnp.transpose(x) for x in (delays, dir_delay, res_delay, iter_delay)
    )

    terms, turn, small, gather, scatter, model_local = pl.pallas_call(
        lambda *refs: station_kernel(*refs, channels=channels, blocks=blocks),
        out_shape=(
            shape(16 * owned, width),
            shape(4 * owned, width),
            shape(3, 2, owned),
            shape(2 * rows, 128, dtype=bf16),
            shape(slots, 2 * rows, dtype=bf16),
            shape(8 * rows, width, dtype=bf16),
        ),
        in_specs=[hbm()] * 9,
        out_specs=(vmem(),) * 6,
        scratch_shapes=[
            pltpu.VMEM((owned, 8, width), f32),
            pltpu.VMEM((owned, 8, width), f32),
            pltpu.VMEM((2, owned), f32),
            pltpu.VMEM((2, rows), jnp.int32),
            pltpu.VMEM((16 * owned, width), f32),
            pltpu.SemaphoreType.DMA((9,)),
        ],
        compiler_params=params(4),
        name="station_terms",
    )(
        *(
            pltpu.with_memory_space_constraint(x, pltpu.HBM)
            for x in (
                gains, dir_band, delays_t, dir_delay_t, res_delay_t, iter_delay_t,
                antenna1.reshape(1, rows), antenna2.reshape(1, rows), model.reshape(rows * 8, width),
            )
        )
    )

    even_groups = [[i, i + 1] for i in range(0, blocks, 2)]
    half = blocks // 2
    groups = [[i, i + 1, i + half, (i + 1 + half) % blocks] for i in range(1, half, 2)]

    def exchange(to_even, to_group):
        count = to_group.shape[1]
        group = lax.all_to_all(
            to_group.reshape(4 * count, width), base, 0, 0, axis_index_groups=groups, tiled=True
        )
        even = lax.all_gather(to_even, base, axis_index_groups=even_groups)
        return even, group.reshape(4, count, width)

    far_pairs = [(i, (i + half) % blocks) for i in range(blocks)]
    odd_pairs = [(i, (i + 1) % blocks if i % 2 else (i - 1) % blocks) for i in range(blocks)]
    from_far = lax.ppermute(terms, base, far_pairs)
    from_odd = lax.ppermute(terms, base, odd_pairs)
    from_even = lax.all_gather(terms, base, axis_index_groups=even_groups)

    to_even, to_group = pl.pallas_call(
        lambda *refs: baseline_kernel(*refs, factor=factor, blocks=blocks),
        out_shape=(shape(8 * owned, width), shape(4, 8 * owned, width)),
        in_specs=[vmem()] * 7,
        out_specs=(vmem(),) * 2,
        scratch_shapes=[
            pltpu.VMEM((slots, 16 * width), f32),
            pltpu.VMEM((2 * rows, 16 * width), f32),
            pltpu.VMEM((2 * rows, 8 * width), f32),
            pltpu.VMEM((8, rows, width), f32),
        ],
        compiler_params=params(24),
        name="baselines",
    )(terms, from_even, from_odd, from_far, model_local, gather, scatter)

    curv, row = pl.pallas_call(
        lambda *refs: curvature_kernel(*refs, channels=channels),
        out_shape=(shape(owned, 8, width), shape(across * lines, width)),
        in_specs=[vmem()] * 7,
        out_specs=(vmem(), vmem()),
        compiler_params=params(4),
        name="curvature",
    )(*exchange(to_even, to_group), terms, turn, small, dir_band, res_band)

    row = lax.all_to_all(row, ("x", "z"), 0, 0, tiled=True)
    row = pl.pallas_call(
        lambda *refs: line_kernel(*refs, across=across),
        out_shape=shape(rings * cores, width),
        in_specs=[vmem()],
        out_specs=vmem(),
        compiler_params=params(4),
        name="line_sums",
    )(row)
    everyone = lax.all_to_all(row, ("y", "core"), 0, 0, tiled=True)

    outs = pl.pallas_call(
        lambda *refs: update_kernel(*refs, across=across),
        out_shape=(
            shape(owned, 8, width),
            shape(2, owned),
            shape(owned, 8, width),
            shape(2, owned),
            shape(owned, 8, width),
            shape(2, owned),
        ),
        in_specs=[vmem()] * 6,
        out_specs=(vmem(),) * 6,
        compiler_params=params(4),
        name="update",
    )(everyone, curv, small, dir_band, res_band, iter_band)
    return (
        outs[0],
        jnp.transpose(outs[1]),
        outs[2],
        jnp.transpose(outs[3]),
        outs[4],
        jnp.transpose(outs[5]),
    )


def solution(mesh):
    cores, across = 2, 4
    blocks, chans = mesh.shape["base"], mesh.shape["chan"]
    split = Mesh(
        mesh.devices.reshape(blocks // across, across, chans // cores, cores), ("y", "x", "z", "core")
    )
    base, chan = ("y", "x"), ("z", "core")
    band = P(base, None, chan)
    delay = P(base, None)
    one = P(base)
    return jax.shard_map(
        body,
        mesh=split,
        in_specs=(band, delay, band, one, one, band, delay, band, delay, band, delay),
        out_specs=(band, delay) * 3,
        check_vma=False,
    )
```

```python
import math

import jax
import jax.numpy as jnp
from jax import lax
from jax.experimental import pallas as pl
from jax.experimental.pallas import tpu as pltpu
from jax.sharding import Mesh
from jax.sharding import PartitionSpec as P

full_turn = 2.0 * math.pi
damping_weight = 0.5

f32 = jnp.float32
bf16 = jnp.bfloat16


def vmem():
    return pl.BlockSpec(memory_space=pltpu.VMEM)


def hbm():
    return pl.BlockSpec(memory_space=pltpu.HBM)


def params(mib):
    return pltpu.CompilerParams(vmem_limit_bytes=int(mib * 1024 * 1024))


def shape(*dims, dtype=f32):
    return jax.ShapeDtypeStruct(dims, dtype)


def base_index():
    return lax.axis_index("y") * lax.axis_size("x") + lax.axis_index("x")


def group_place(blocks):
    block = base_index()
    first = jnp.where(block % 2 == 1, block, (block + blocks - 1) % blocks)
    return 1 - block % 2 + 2 * jnp.where(first >= blocks // 2, 1, 0)


def chan_index():
    return lax.axis_index("z") * lax.axis_size("core") + lax.axis_index("core")


def frequencies(chan, width, channels):
    index = lax.broadcasted_iota(jnp.int32, (1, width), 1) + chan * width
    return (index.astype(f32) + 0.5) / channels - 0.5


def column(row_ref):
    count = row_ref.shape[1]
    eye = lax.broadcasted_iota(jnp.int32, (count, count), 0) == lax.broadcasted_iota(
        jnp.int32, (count, count), 1
    )
    parts = [
        jnp.sum(
            jnp.where(eye, jnp.broadcast_to(row_ref[a : a + 1, :], (count, count)), 0.0),
            axis=1,
            keepdims=True,
        )
        for a in range(2)
    ]
    return jnp.concatenate(parts, axis=0)


def pick_stations(ids, gather_ref, scatter_ref, *, owned, blocks):
    rows = ids.shape[1]
    slots = 4 * owned
    slot = lax.broadcasted_iota(jnp.int32, (slots, 2 * rows), 0)
    kind = slot // owned
    block = base_index()
    turn_up = 1 - 2 * (block % 2)
    offset = jnp.where(kind == 0, 0, jnp.where(kind == 1, turn_up, jnp.where(kind == 2, -turn_up, blocks // 2)))
    station = ((block + offset + blocks) % blocks) * owned + slot % owned
    both = jnp.concatenate([ids[0:1, :], ids[1:2, :]], axis=1)
    pick = jnp.where(station == both, 1.0, 0.0)
    filled = jnp.concatenate([pick] * 3 + [jnp.zeros((128 - 3 * slots, 2 * rows), f32)], axis=0)
    scatter_ref[...] = pick.astype(bf16)
    gather_ref[...] = jnp.transpose(filled).astype(bf16)


def station_kernel(
    gains_hbm, band_hbm, delays_hbm, move_hbm, left_hbm, iter_hbm, first_hbm, second_hbm, model_hbm,
    terms_ref, turn_ref, small_ref, gather_ref, scatter_ref, model_ref,
    gains_ref, band_ref, delays_ref, ids, packed, sems, *, channels, blocks
):
    owned, _, width = gains_ref.shape
    rows = ids.shape[1]
    half = 2 * owned
    pairs = [
        (first_hbm, ids.at[0:1]),
        (second_hbm, ids.at[1:2]),
        (delays_hbm, delays_ref),
        (move_hbm, small_ref.at[0]),
        (gains_hbm, gains_ref),
        (band_hbm, band_ref),
    ]
    parts = 1
    share = 8 * rows // parts
    for k in range(parts):
        at = pl.ds(k * share, share)
        pairs.append((model_hbm.at[at], model_ref.at[at]))
    pairs += [(left_hbm, small_ref.at[1]), (iter_hbm, small_ref.at[2])]
    copies = [pltpu.make_async_copy(a, b, sems.at[k]) for k, (a, b) in enumerate(pairs)]
    for copy in copies:
        copy.start()
    copies[0].wait()
    copies[1].wait()
    pick_stations(ids, gather_ref, scatter_ref, owned=owned, blocks=blocks)
    copies[2].wait()
    copies[3].wait()
    delay_scale = channels ** (-0.5)
    freq = frequencies(chan_index(), width, channels)
    phase = full_turn * column(delays_ref) * freq
    rate = full_turn * delay_scale * column(small_ref.at[0]) * freq
    cosine = jnp.cos(phase)
    sine = jnp.sin(phase)
    turn_ref[0:half, :] = cosine
    turn_ref[half : 2 * half, :] = sine
    copies[4].wait()
    copies[5].wait()
    for j in range(8):
        packed[j * owned : (j + 1) * owned, :] = gains_ref[:, j, :]
        packed[(8 + j) * owned : (9 + j) * owned, :] = band_ref[:, j, :]
    for r in range(2):
        re = slice(r * half, (r + 1) * half)
        im = slice((2 + r) * half, (3 + r) * half)
        move_re = slice((4 + r) * half, (5 + r) * half)
        move_im = slice((6 + r) * half, (7 + r) * half)
        jones_re = cosine * packed[re, :] - sine * packed[im, :]
        jones_im = cosine * packed[im, :] + sine * packed[re, :]
        terms_ref[re, :] = jones_re
        terms_ref[im, :] = jones_im
        terms_ref[move_re, :] = (
            cosine * packed[move_re, :] - sine * packed[move_im, :] - rate * jones_im
        )
        terms_ref[move_im, :] = (
            cosine * packed[move_im, :] + sine * packed[move_re, :] + rate * jones_re
        )
    for copy in copies[6:]:
        copy.wait()


def times(a, b):
    out = []
    for r in range(2):
        for c in range(2):
            out.append(
                a[r * 2] * b[c] - a[4 + r * 2] * b[4 + c] + a[r * 2 + 1] * b[2 + c] - a[5 + r * 2] * b[6 + c]
            )
    for r in range(2):
        for c in range(2):
            out.append(
                a[r * 2] * b[4 + c] + a[4 + r * 2] * b[c] + a[r * 2 + 1] * b[6 + c] + a[5 + r * 2] * b[2 + c]
            )
    return out


def times_adjoint(a, b):
    out = []
    for r in range(2):
        for c in range(2):
            out.append(
                a[r * 2] * b[c * 2]
                + a[4 + r * 2] * b[4 + c * 2]
                + a[r * 2 + 1] * b[c * 2 + 1]
                + a[5 + r * 2] * b[5 + c * 2]
            )
    for r in range(2):
        for c in range(2):
            out.append(
                a[4 + r * 2] * b[c * 2]
                - a[r * 2] * b[4 + c * 2]
                + a[5 + r * 2] * b[c * 2 + 1]
                - a[r * 2 + 1] * b[5 + c * 2]
            )
    return out


def adjoint_times(a, b):
    out = []
    for r in range(2):
        for c in range(2):
            out.append(
                a[r] * b[c] + a[4 + r] * b[4 + c] + a[2 + r] * b[2 + c] + a[6 + r] * b[6 + c]
            )
    for r in range(2):
        for c in range(2):
            out.append(
                a[r] * b[4 + c] - a[4 + r] * b[c] + a[2 + r] * b[6 + c] - a[6 + r] * b[2 + c]
            )
    return out


def baseline_kernel(
    own_ref, even_ref, odd_ref, far_ref, model_ref, gather_ref, scatter_ref,
    even_out, group_out, table, picked, grads, model_parts, *, factor, blocks
):
    _, rows, width = model_parts.shape
    slots = table.shape[0]
    owned = slots // 4
    group = 32
    size = 8 * group
    place = group_place(blocks)
    odd_place = place + 1 - 2 * (place % 2)
    far_place = (place + 2) % 4
    partner = even_ref.at[1 - base_index() % 2]
    sources = (own_ref, partner, odd_ref, far_ref)
    for k, ref in enumerate(sources):
        for j in range(16):
            table[k * owned : (k + 1) * owned, j * width : (j + 1) * width] = ref[
                j * owned : (j + 1) * owned, :
            ]
    exact = table[...]
    high = exact.astype(bf16)
    rest = exact - high.astype(f32)
    middle = rest.astype(bf16)
    low = (rest - middle.astype(f32)).astype(bf16)
    split = jnp.concatenate(
        [high, middle, low, jnp.zeros((128 - 3 * slots, exact.shape[1]), bf16)], axis=0
    )
    out_row = lax.broadcasted_iota(jnp.int32, (size, size), 0)
    in_row = lax.broadcasted_iota(jnp.int32, (size, size), 1)
    wanted = (out_row % group) * 8 + out_row // group
    shuffle = jnp.where(in_row == wanted, 1.0, 0.0).astype(bf16)
    step = 2 * width
    cols = [slice(j * width, (j + 1) * width) for j in range(16)]
    stage = rows // 2
    def load(first):
        for g in range(first // group, (first + stage) // group):
            part = jnp.dot(
                shuffle, model_ref[g * size : (g + 1) * size, :], preferred_element_type=f32
            )
            for j in range(8):
                model_parts[j, g * group : (g + 1) * group, :] = part[j * group : (j + 1) * group, :]
        for base in (first, rows + first):
            pick = gather_ref[base : base + stage, :]
            for n in range(0, 16 * width, step):
                picked[base : base + stage, n : n + step] = jnp.dot(pick, split[:, n : n + step], preferred_element_type=f32)

    def chunk(i):
        at = slice(i * 8, i * 8 + 8)
        at_q = slice(rows + i * 8, rows + i * 8 + 8)
        model = [model_parts[j, at, :] for j in range(8)]
        right = times_adjoint(model, [picked[at_q, c] for c in cols[:8]])
        left = times([picked[at, c] for c in cols[:8]], model)
        one = times([picked[at, c] for c in cols[8:]], right)
        two = times_adjoint(left, [picked[at_q, c] for c in cols[8:]])
        change = [a + b for a, b in zip(one, two)]
        for c, value in zip(cols, times_adjoint(change, right)):
            grads[at, c] = value
        for c, value in zip(cols, adjoint_times(change, left)):
            grads[at_q, c] = value

    def collect(first):
        for n in range(0, 8 * width, step):
            total = None
            for base in (first, rows + first):
                value = grads[base : base + stage, n : n + step]
                sel = scatter_ref[:, base : base + stage]
                high = value.astype(bf16)
                low = (value - high.astype(f32)).astype(bf16)
                part = jnp.dot(sel, high, preferred_element_type=f32) + jnp.dot(
                    sel, low, preferred_element_type=f32
                )
                total = part if total is None else total + part
            if first:
                table[:, n : n + step] = table[:, n : n + step] + factor * total
            else:
                table[:, n : n + step] = factor * total

    load(0)
    for first in range(0, rows, stage):
        if first + stage < rows:
            load(first + stage)
        for i in range(first // 8, (first + stage) // 8):
            chunk(i)
        collect(first)
    group_out[(odd_place + 2) % 4] = jnp.zeros(even_out.shape, f32)
    sinks = (group_out.at[place], even_out, group_out.at[odd_place], group_out.at[far_place])
    for k, ref in enumerate(sinks):
        for j in range(8):
            ref[j * owned : (j + 1) * owned, :] = table[
                k * owned : (k + 1) * owned, j * width : (j + 1) * width
            ]


def curvature_kernel(
    even_ref, group_ref, terms_ref, turn_ref, small_ref, band_ref, res_ref,
    curv_ref, row_ref, *, channels
):
    owned, _, width = band_ref.shape
    half = 2 * owned
    delay_scale = channels ** (-0.5)
    freq = frequencies(chan_index(), width, channels)
    cosine = turn_ref[0:half, :]
    sine = turn_ref[half : 2 * half, :]
    total = even_ref[1 - base_index() % 2]
    for k in range(4):
        total = total + group_ref[k]
    moved = jnp.zeros((half, width), f32)
    for r in range(2):
        re = slice(r * half, (r + 1) * half)
        im = slice((2 + r) * half, (3 + r) * half)
        grad_re, grad_im = total[re, :], total[im, :]
        moved = moved + (terms_ref[re, :] * grad_im - terms_ref[im, :] * grad_re)
        band_re = cosine * grad_re + sine * grad_im
        band_im = cosine * grad_im - sine * grad_re
        for a in range(2):
            rows = slice(a * owned, (a + 1) * owned)
            j = 2 * r + a
            curv_ref[:, j, :] = band_re[rows, :] + damping_weight * band_ref[:, j, :]
            curv_ref[:, 4 + j, :] = band_im[rows, :] + damping_weight * band_ref[:, 4 + j, :]
    moved = moved * (full_turn * delay_scale * freq)
    curv, band, res = curv_ref[...], band_ref[...], res_ref[...]
    scalars = [
        jnp.sum(jnp.sum(x, axis=0), axis=0, keepdims=True)
        for x in (res * res, res * curv, curv * curv, band * curv)
    ]
    sums = jnp.sum(
        jnp.concatenate([moved] + scalars + [jnp.zeros((4, width), f32)], axis=0), axis=1, keepdims=True
    )
    here = jnp.where(lax.axis_index("z") == 0, 1.0, 0.0)
    values = jnp.concatenate(
        [sums] + [here * column(small_ref.at[0]), here * column(small_ref.at[1])],
        axis=0,
    )
    count = values.shape[0]
    diagonal = lax.broadcasted_iota(jnp.int32, (count, width), 0) == lax.broadcasted_iota(
        jnp.int32, (count, width), 1
    )
    row = jnp.sum(
        jnp.where(diagonal, jnp.broadcast_to(values, (count, width)), 0.0), axis=0, keepdims=True
    )
    row_ref[...] = jnp.broadcast_to(row, row_ref.shape)


def line_kernel(rows_ref, out_ref, *, across):
    count, width = rows_ref.shape
    lines, part = count // across, width // across
    lane = lax.broadcasted_iota(jnp.int32, (1, width), 1)
    total = jnp.zeros((1, width), f32)
    for x in range(across):
        line = jnp.sum(rows_ref[x * lines : (x + 1) * lines, :], axis=0, keepdims=True)
        line = jnp.where(lane < part, line, 0.0)
        total = total + (pltpu.roll(line, x * part, 1) if x else line)
    out_ref[...] = jnp.broadcast_to(total, out_ref.shape)


def update_kernel(
    rows_ref, curv_ref, small_ref, band_ref, res_ref, iter_ref,
    iter_out, iter_delay_out, res_out, res_delay_out, dir_out, dir_delay_out, *, across
):
    rows = rows_ref[...]
    count, width = rows.shape
    owned = band_ref.shape[0]
    half = 2 * owned
    sums = jnp.sum(rows, axis=0, keepdims=True)
    part = width // across
    lane = lax.broadcasted_iota(jnp.int32, (1, width), 1) % part

    def scalar(x):
        return jnp.sum(x, axis=1, keepdims=True)

    pair = rows + pltpu.roll(rows, count - 1, 0)
    moves = pltpu.roll(rows, width - 16, 1)
    lefts = pltpu.roll(rows, width - 24, 1)
    curves = pair + damping_weight * moves
    valid = (lax.broadcasted_iota(jnp.int32, (count, width), 0) % 2 == 0) & (
        lax.broadcasted_iota(jnp.int32, (count, width), 1) % part < half
    )

    products = (lefts * lefts, lefts * curves, curves * curves, moves * curves)
    totals = scalar(
        jnp.concatenate(
            [
                jnp.where(lane == half + k, sums, 0.0)
                + jnp.sum(jnp.where(valid, x, 0.0), axis=0, keepdims=True)
                for k, x in enumerate(products)
            ],
            axis=0,
        )
    )
    squares, cross, norm, curvature = (totals[k : k + 1] for k in range(4))
    alpha = squares / curvature
    fresh = squares + alpha * (alpha * norm - 2.0 * cross)
    ratio = fresh / squares

    band, curv = band_ref[...], curv_ref[...]
    alpha3 = alpha.reshape(1, 1, 1)
    ratio3 = ratio.reshape(1, 1, 1)
    iter_out[...] = iter_ref[...] + alpha3 * band
    new_res = res_ref[...] - alpha3 * curv
    res_out[...] = new_res
    dir_out[...] = new_res + ratio3 * band

    mine = lax.broadcasted_iota(jnp.int32, (count, width), 0) == 2 * lax.axis_index("y")
    line = jnp.sum(jnp.where(mine, pair, 0.0), axis=0, keepdims=True)
    own = jnp.zeros((1, half), f32)
    for x in range(across):
        own = own + jnp.where(lax.axis_index("x") == x, line[:, x * part : x * part + half], 0.0)
    own = jnp.concatenate([own[:, 0:owned], own[:, owned:half]], axis=0)
    move = small_ref[0]
    iter_delay_out[...] = small_ref[2] + alpha * move
    new_left = small_ref[1] - alpha * (own + damping_weight * move)
    res_delay_out[...] = new_left
    dir_delay_out[...] = new_left + ratio * move


def body(
    gains,
    delays,
    model,
    antenna1,
    antenna2,
    dir_band,
    dir_delay,
    res_band,
    res_delay,
    iter_band,
    iter_delay,
):
    owned, _, width = gains.shape
    rows = model.shape[0]
    rings, lines = lax.axis_size("y"), lax.axis_size("z")
    across, cores = lax.axis_size("x"), lax.axis_size("core")
    blocks = rings * across
    base = ("y", "x")
    channels = width * lines * cores
    slots = 4 * owned
    factor = owned / (2.0 * rows)
    delays_t, dir_delay_t, res_delay_t, iter_delay_t = (
        jnp.transpose(x) for x in (delays, dir_delay, res_delay, iter_delay)
    )

    terms, turn, small, gather, scatter, model_local = pl.pallas_call(
        lambda *refs: station_kernel(*refs, channels=channels, blocks=blocks),
        out_shape=(
            shape(16 * owned, width),
            shape(4 * owned, width),
            shape(3, 2, owned),
            shape(2 * rows, 128, dtype=bf16),
            shape(slots, 2 * rows, dtype=bf16),
            shape(8 * rows, width, dtype=bf16),
        ),
        in_specs=[hbm()] * 9,
        out_specs=(vmem(),) * 6,
        scratch_shapes=[
            pltpu.VMEM((owned, 8, width), f32),
            pltpu.VMEM((owned, 8, width), f32),
            pltpu.VMEM((2, owned), f32),
            pltpu.VMEM((2, rows), jnp.int32),
            pltpu.VMEM((16 * owned, width), f32),
            pltpu.SemaphoreType.DMA((9,)),
        ],
        compiler_params=params(4),
        name="station_terms",
    )(
        *(
            pltpu.with_memory_space_constraint(x, pltpu.HBM)
            for x in (
                gains, dir_band, delays_t, dir_delay_t, res_delay_t, iter_delay_t,
                antenna1.reshape(1, rows), antenna2.reshape(1, rows), model.reshape(rows * 8, width),
            )
        )
    )

    even_groups = [[i, i + 1] for i in range(0, blocks, 2)]
    half = blocks // 2
    groups = [[i, i + 1, i + half, (i + 1 + half) % blocks] for i in range(1, half, 2)]

    def exchange(to_even, to_group):
        count = to_group.shape[1]
        group = lax.all_to_all(
            to_group.reshape(4 * count, width), base, 0, 0, axis_index_groups=groups, tiled=True
        )
        even = lax.all_gather(to_even, base, axis_index_groups=even_groups)
        return even, group.reshape(4, count, width)

    far_pairs = [(i, (i + half) % blocks) for i in range(blocks)]
    odd_pairs = [(i, (i + 1) % blocks if i % 2 else (i - 1) % blocks) for i in range(blocks)]
    from_far = lax.ppermute(terms, base, far_pairs)
    from_odd = lax.ppermute(terms, base, odd_pairs)
    from_even = lax.all_gather(terms, base, axis_index_groups=even_groups)

    to_even, to_group = pl.pallas_call(
        lambda *refs: baseline_kernel(*refs, factor=factor, blocks=blocks),
        out_shape=(shape(8 * owned, width), shape(4, 8 * owned, width)),
        in_specs=[vmem()] * 7,
        out_specs=(vmem(),) * 2,
        scratch_shapes=[
            pltpu.VMEM((slots, 16 * width), f32),
            pltpu.VMEM((2 * rows, 16 * width), f32),
            pltpu.VMEM((2 * rows, 8 * width), f32),
            pltpu.VMEM((8, rows, width), f32),
        ],
        compiler_params=params(24),
        name="baselines",
    )(terms, from_even, from_odd, from_far, model_local, gather, scatter)

    curv, row = pl.pallas_call(
        lambda *refs: curvature_kernel(*refs, channels=channels),
        out_shape=(shape(owned, 8, width), shape(across * lines, width)),
        in_specs=[vmem()] * 7,
        out_specs=(vmem(), vmem()),
        compiler_params=params(4),
        name="curvature",
    )(*exchange(to_even, to_group), terms, turn, small, dir_band, res_band)

    row = lax.all_to_all(row, ("x", "z"), 0, 0, tiled=True)
    row = pl.pallas_call(
        lambda *refs: line_kernel(*refs, across=across),
        out_shape=shape(rings * cores, width),
        in_specs=[vmem()],
        out_specs=vmem(),
        compiler_params=params(4),
        name="line_sums",
    )(row)
    everyone = lax.all_to_all(row, ("y", "core"), 0, 0, tiled=True)

    outs = pl.pallas_call(
        lambda *refs: update_kernel(*refs, across=across),
        out_shape=(
            shape(owned, 8, width),
            shape(2, owned),
            shape(owned, 8, width),
            shape(2, owned),
            shape(owned, 8, width),
            shape(2, owned),
        ),
        in_specs=[vmem()] * 6,
        out_specs=(vmem(),) * 6,
        compiler_params=params(4),
        name="update",
    )(everyone, curv, small, dir_band, res_band, iter_band)
    return (
        outs[0],
        jnp.transpose(outs[1]),
        outs[2],
        jnp.transpose(outs[3]),
        outs[4],
        jnp.transpose(outs[5]),
    )


def solution(mesh):
    cores, across = 2, 4
    blocks, chans = mesh.shape["base"], mesh.shape["chan"]
    split = Mesh(
        mesh.devices.reshape(blocks // across, across, chans // cores, cores), ("y", "x", "z", "core")
    )
    base, chan = ("y", "x"), ("z", "core")
    band = P(base, None, chan)
    delay = P(base, None)
    one = P(base)
    return jax.shard_map(
        body,
        mesh=split,
        in_specs=(band, delay, band, one, one, band, delay, band, delay, band, delay),
        out_specs=(band, delay) * 3,
        check_vma=False,
    )
```
